768 devices in a mesh: section: 2 (over core), dp: 24 (over y_lo, z), mp: 16 (over y_hi, x).
Axes of the slice: x: 4, y: 8 (y_hi: 4, y_lo: 2; y = y_hi * 2 + y_lo), z: 12, core: 2. Of those that a mesh axis runs over, the one named last changes fastest.
Arguments:
- states: bfloat16 [2, 12288, 4096], P('section', 'dp', 'mp')
- proj_weights: bfloat16 [2, 2, 4096, 4096], P('section', None, None, 'mp'), may hold values from -0.09375 to 0.09375
- out_cotangent: bfloat16 [12288, 4096], P('dp', 'mp'), may hold values from -6 to 6
- enc_lengths: int32 [48], P('dp'), may hold values from 64 to 256
- dec_lengths: int32 [48], P('dp'), may hold values from 64 to 256
Outputs:
- state_grads: bfloat16 [2, 12288, 4096], P('section', 'dp', 'mp')
The draws below stay inside these ranges and needn't reach their ends.
All inputs are finite; a program needn't handle non-finite values.
Results may differ from the reference program's by a relative error of at most 0.023.
The reference program's roundings to bfloat16 on the way count: a program that leaves them out, or rounds other values in their place, can miss the bound.
Values may be sent and summed in bfloat16 or wider, within the bound.
No kernel may reach another device: no remote copies, remote signals or barrier semaphores. Data moves between devices by JAX's collectives and lax.ppermute only.
A program may use at most 32 MiB of HBM per device.

```python
import jax
import jax.numpy as jnp
from jax import lax

D = 4096
HEADS = 16
HS = 256
LEN = 256
SEQS = 48
ROWS = 12288
N_MP = 16


def draw_states(key, part):
    key = jax.random.fold_in(key, 11)
    first = jax.random.fold_in(key, 0)
    values = jax.random.normal(first, (2, ROWS, D), jnp.float32)
    return jnp.clip(values, -8.0, 8.0).astype(jnp.bfloat16)


def with_ends(array, stream_key, least, high):
    index_at = [jax.random.randint(jax.random.fold_in(stream_key, axis), (), 0, length) for axis, length in enumerate(array.shape)]
    main_axis = array.shape.index(max(array.shape))
    next_to = index_at[:main_axis] + [(index_at[main_axis] + 1) % array.shape[main_axis]] + index_at[main_axis + 1:]
    return array.at[tuple(index_at)].set(least).at[tuple(next_to)].set(high)


def levels(stream_key, extent, pieces, least, largest):
    factor_of = 1.0
    for axis_at, parts in pieces:
        draws = jax.random.uniform(jax.random.fold_in(jax.random.fold_in(stream_key, 6), axis_at), (parts,), jnp.float32, least / len(pieces), largest / len(pieces))
        factor_of = factor_of * jnp.repeat(jnp.exp(draws), extent[axis_at] // parts).reshape((-1,) + (1,) * (len(extent) - 1 - axis_at))
    return factor_of


def noise(key, extent, scale, most, shards=(), held_as=jnp.bfloat16):
    gain = levels(key, extent, shards, -0.22, 0.18) if shards else 1.0
    entries = jax.random.normal(key, extent, jnp.float32) * scale * gain
    return jnp.minimum(jnp.maximum(entries, -most), most).astype(held_as)


def setup_inputs(seed: int = 0) -> dict:
    key_list = jax.random.split(jax.random.key(seed), 6)
    return {
        "states": draw_states(jax.random.fold_in(key_list[5], 71), 0),
        "proj_weights": noise(key_list[1], (2, 2, D, HEADS * HS), D ** -0.5, 0.09375, ((0, 2), (3, 16))),
        "out_cotangent": noise(key_list[2], (ROWS, D), 1.0, 6.0, ((0, 24), (1, 16))),
        "enc_lengths": with_ends(jax.random.randint(key_list[3], (SEQS,), LEN // 4, LEN + 1), jax.random.fold_in(key_list[3], 1), LEN // 4, LEN).astype(jnp.int32),
        "dec_lengths": with_ends(jax.random.randint(key_list[4], (SEQS,), LEN // 4, LEN + 1), jax.random.fold_in(key_list[4], 1), LEN // 4, LEN).astype(jnp.int32),
    }


def attend(queries, keys, values, out_grad, enc_lengths, dec_lengths):
    shape4 = (SEQS, LEN, HEADS, HS)
    q4 = queries.reshape(shape4).astype(jnp.float32)
    k4 = keys.reshape(shape4).astype(jnp.float32)
    v4 = values.reshape(shape4).astype(jnp.float32)
    g4 = out_grad.reshape(shape4)
    slots = jnp.arange(LEN, dtype=jnp.int32)
    key_live = slots[None, :] < enc_lengths[:, None]
    query_live = slots[None, :] < dec_lengths[:, None]
    g4 = jnp.where(query_live[:, :, None, None], g4, jnp.zeros_like(g4)).astype(jnp.float32)
    scale = 1.0 / (HS ** 0.5)
    scores = jnp.einsum("sqhc,skhc->shqk", q4, k4) * scale
    scores = jnp.where(key_live[:, None, None, :], scores, -1e30)
    top = jnp.max(scores, axis=-1, keepdims=True)
    expd = jnp.exp(scores - top)
    probs = expd / jnp.sum(expd, axis=-1, keepdims=True)
    probs_b = probs.astype(jnp.bfloat16).astype(jnp.float32)
    value_grad = jnp.einsum("shqk,sqhc->skhc", probs_b, g4).astype(jnp.bfloat16)
    prob_grad = jnp.einsum("sqhc,skhc->shqk", g4, v4)
    delta = jnp.sum(probs * prob_grad, axis=-1, keepdims=True)
    score_grad = probs * (prob_grad - delta)
    sg_b = score_grad.astype(jnp.bfloat16).astype(jnp.float32)
    query_grad = (jnp.einsum("shqk,skhc->sqhc", sg_b, k4) * scale).astype(jnp.bfloat16)
    key_grad = (jnp.einsum("shqk,sqhc->skhc", sg_b, q4) * scale).astype(jnp.bfloat16)
    flat = (ROWS, HEADS * HS)
    return query_grad.reshape(flat), key_grad.reshape(flat), value_grad.reshape(flat)


def group_sum(pairs):
    width = HEADS // N_MP * HS

    def step(total, group):
        start = group * width
        term = jnp.zeros((ROWS, D), jnp.float32)
        for grads, weight in pairs:
            g_part = lax.dynamic_slice_in_dim(grads, start, width, 1)
            w_part = lax.dynamic_slice_in_dim(weight, start, width, 1)
            term = term + lax.dot_general(g_part, w_part, (((1,), (1,)), ((), ())), preferred_element_type=jnp.float32)
        term = term.astype(jnp.bfloat16).astype(jnp.float32)
        return total + term, None

    total, _ = lax.scan(step, jnp.zeros((ROWS, D), jnp.float32), jnp.arange(N_MP, dtype=jnp.int32))
    return total.astype(jnp.bfloat16)


def reference(states, proj_weights, out_cotangent, enc_lengths, dec_lengths):
    w_key, w_value = proj_weights[0, 0], proj_weights[0, 1]
    w_query, w_out_t = proj_weights[1, 0], proj_weights[1, 1]
    keys = jnp.dot(states[0], w_key, preferred_element_type=jnp.float32).astype(jnp.bfloat16)
    values = jnp.dot(states[0], w_value, preferred_element_type=jnp.float32).astype(jnp.bfloat16)
    queries = jnp.dot(states[1], w_query, preferred_element_type=jnp.float32).astype(jnp.bfloat16)
    out_grad = jnp.dot(out_cotangent, w_out_t, preferred_element_type=jnp.float32).astype(jnp.bfloat16)
    query_grad, key_grad, value_grad = attend(queries, keys, values, out_grad, enc_lengths, dec_lengths)
    enc_grad = group_sum([(key_grad, w_key), (value_grad, w_value)])
    dec_grad = group_sum([(query_grad, w_query)])
    return jnp.stack([enc_grad, dec_grad])
```

```python
import jax
import jax.numpy as jnp
from jax import lax
from jax.experimental import pallas as pl
from jax.experimental.pallas import tpu as pltpu
from jax.sharding import PartitionSpec as P

HS = 256
SIDE = 4
F32 = jnp.float32
BF16 = jnp.bfloat16
SWAP = [(0, 1), (1, 0)]


def shift_x(block, step):
    route = [(y * SIDE + x, y * SIDE + (x + step) % SIDE) for y in range(SIDE) for x in range(SIDE)]
    return lax.ppermute(block, "mp", route)


def shift_y(block, step):
    route = [(y * SIDE + x, (y + step) % SIDE * SIDE + x) for y in range(SIDE) for x in range(SIDE)]
    return lax.ppermute(block, "mp", route)


def cat(*parts):
    return jnp.concatenate(parts, axis=0)


def project(blocks, places, sec, own_w, other_w, total):
    rows = 3 * HS
    count = len(places)
    scalars = jnp.stack([*places, sec]).astype(jnp.int32)
    first = total is None

    def body(scalar_ref, x_ref, u_ref, r_ref, *rest):
        out_ref = rest[-1]
        step = pl.program_id(0)
        shift = pl.multiple_of(scalar_ref[count] * HS, HS)

        @pl.when(step == 0)
        def _():
            if first:
                out_ref[...] = jnp.zeros_like(out_ref)
            else:
                out_ref[...] = rest[0][...]

        low = x_ref[pl.ds(shift, HS), :]
        mid = x_ref[pl.ds(shift + HS, HS), :]
        out_ref[0] += jnp.dot(x_ref[:HS, :], u_ref[0], preferred_element_type=F32)
        out_ref[1] += jnp.dot(low, u_ref[1], preferred_element_type=F32)
        out_ref[2] += jnp.dot(mid, r_ref[0], preferred_element_type=F32)
        out_ref[3] += jnp.dot(x_ref[2 * HS :, :], r_ref[1], preferred_element_type=F32)

    whole = pl.BlockSpec((4, HS, HS), lambda i, s: (0, 0, 0))
    weight = pl.BlockSpec((2, HS, HS), lambda i, s: (0, s[i], 0))
    return pl.pallas_call(
        body,
        out_shape=jax.ShapeDtypeStruct((4, HS, HS), F32),
        grid_spec=pltpu.PrefetchScalarGridSpec(
            num_scalar_prefetch=1,
            grid=(count,),
            in_specs=[pl.BlockSpec((rows, HS), lambda i, s: (i, 0)), weight, weight] + ([] if first else [whole]),
            out_specs=whole,
        ),
        cost_estimate=pl.CostEstimate(
            flops=count * 8 * HS**3, bytes_accessed=count * 7 * HS * HS * 2, transcendentals=0
        ),
    )(scalars, blocks, own_w, other_w, *([] if first else [total]))


def attend_and_spread(total, sec, enc_lengths, dec_lengths, own_w, other_w):
    scale = 1.0 / HS**0.5
    groups = own_w.shape[1] // HS
    scalars = jnp.stack([sec, enc_lengths[sec], dec_lengths[sec]]).astype(jnp.int32)

    def body(scalar_ref, t_ref, u_ref, r_ref, out_ref, g_ref):
        nt = (((1,), (1,)), ((), ()))
        tn = (((0,), (0,)), ((), ()))

        @pl.when(pl.program_id(0) == 0)
        def _():
            me = scalar_ref[0]
            keys = t_ref[2 * me].astype(BF16)
            values = t_ref[2 * me + 1].astype(BF16)
            queries = t_ref[2 - 2 * me].astype(BF16)
            out_grad = t_ref[3 - 2 * me]
            live_q = lax.broadcasted_iota(jnp.int32, (HS, HS), 0) < scalar_ref[2]
            live_k = lax.broadcasted_iota(jnp.int32, (HS, HS), 1) < scalar_ref[1]
            masked = jnp.where(live_q, out_grad, 0.0).astype(BF16)
            scores = lax.dot_general(queries, keys, nt, preferred_element_type=F32) * scale
            scores = jnp.where(live_k, scores, -1e30)
            top = jnp.max(scores, axis=-1, keepdims=True)
            expd = jnp.exp(scores - top)
            probs = expd / jnp.sum(expd, axis=-1, keepdims=True)
            value_grad = lax.dot_general(probs.astype(BF16), masked, tn, preferred_element_type=F32).astype(BF16)
            prob_grad = lax.dot_general(masked, values, nt, preferred_element_type=F32)
            delta = jnp.sum(probs * prob_grad, axis=-1, keepdims=True)
            sg = (probs * (prob_grad - delta)).astype(BF16)
            query_grad = (jnp.dot(sg, keys, preferred_element_type=F32) * scale).astype(BF16)
            key_grad = (lax.dot_general(sg, queries, tn, preferred_element_type=F32) * scale).astype(BF16)
            g_ref[2 * me] = key_grad
            g_ref[2 * me + 1] = value_grad
            g_ref[2 - 2 * me] = query_grad
            g_ref[3 - 2 * me] = jnp.zeros_like(query_grad)

        for slot, w_ref in ((0, u_ref), (1, r_ref)):
            term = lax.dot_general(g_ref[2 * slot], w_ref[0], nt, preferred_element_type=F32)
            term += lax.dot_general(g_ref[2 * slot + 1], w_ref[1], nt, preferred_element_type=F32)
            out_ref[slot, 0] = term.astype(BF16)

    weight = pl.BlockSpec((2, HS, HS), lambda i, s: (0, i, 0))
    return pl.pallas_call(
        body,
        out_shape=jax.ShapeDtypeStruct((2, groups, HS, HS), BF16),
        grid_spec=pltpu.PrefetchScalarGridSpec(
            num_scalar_prefetch=1,
            grid=(groups,),
            in_specs=[pl.BlockSpec((4, HS, HS), lambda i, s: (0, 0, 0)), weight, weight],
            out_specs=pl.BlockSpec((2, 1, HS, HS), lambda i, s: (0, i, 0, 0)),
            scratch_shapes=[pltpu.VMEM((4, HS, HS), BF16)],
        ),
        cost_estimate=pl.CostEstimate(
            flops=groups * 8 * HS**3, bytes_accessed=groups * 6 * HS * HS * 2, transcendentals=HS * HS
        ),
    )(scalars, total, own_w, other_w)


def local(states, proj_weights, out_cotangent, enc_lengths, dec_lengths):
    sec = lax.axis_index("section")
    me = lax.axis_index("mp")
    my_y, my_x = me // SIDE, me % SIDE

    def place(dy, dx):
        return (my_y + dy) % SIDE * SIDE + (my_x + dx) % SIDE

    own_w = proj_weights[0]
    rows = states[0].reshape(2, HS, HS)
    mine = lax.dynamic_index_in_dim(rows, sec, 0, keepdims=False)
    partner = lax.ppermute(lax.dynamic_index_in_dim(rows, 1 - sec, 0, keepdims=False), "section", SWAP)
    other_w = lax.ppermute(own_w, "section", SWAP)
    cotangent = lax.dynamic_slice_in_dim(out_cotangent, sec * HS, HS, 0)
    is_first = sec == 0
    c0 = cat(mine, jnp.where(is_first, partner, cotangent), jnp.where(is_first, cotangent, partner))
    n = c0.shape[0]
    h = n // 2

    up1, down1 = shift_y(c0, 1), shift_y(c0, -1)
    right0, left0 = shift_x(c0, 1), shift_x(c0, -1)
    right1 = shift_x(cat(right0[:h], up1, down1), 1)
    left1 = shift_x(cat(left0[h:], up1, down1), -1)
    up2, down2 = shift_y(up1[:h], 1), shift_y(down1[h:], -1)
    right2 = shift_x(cat(right1[h : 2 * h], right1[h + n : 2 * h + n], up2, down2), 1)
    left2 = shift_x(cat(left1[n : n + h], left1[2 * n : 2 * n + h], up2, down2), -1)
    right3, left3 = shift_x(right2[n : n + h], 1), shift_x(left2[n + h :], -1)

    total = project(
        cat(c0, up1, down1, right0, left0),
        [place(0, 0), place(-1, 0), place(1, 0), place(0, -1), place(0, 1)],
        sec, own_w, other_w, None,
    )
    total = project(
        cat(right1[h:], left1[h:], right1[:h], left1[:h], up2, down2),
        [place(-1, -1), place(1, -1), place(-1, 1), place(1, 1), place(0, 2), place(2, 0)],
        sec, own_w, other_w, total,
    )
    total = project(
        cat(right2[:h], left2[:h], right2[h:n], left2[h:n], right2[n:], left2[n:]),
        [place(-1, 2), place(1, 2), place(2, -1), place(2, 1)],
        sec, own_w, other_w, total,
    )
    total = project(cat(right3, left3), [place(2, 2)], sec, own_w, other_w, total)

    terms = attend_and_spread(total, sec, enc_lengths, dec_lengths, own_w, other_w)
    by_section = jnp.where(is_first, terms, terms[::-1])
    arrived = lax.all_to_all(by_section.reshape(32, HS, HS), ("section", "mp"), 0, 0, tiled=True)
    summed = jnp.sum(arrived.reshape(2, 16, HS, HS).astype(F32), axis=1)
    return summed.astype(BF16).reshape(1, 2 * HS, HS)


def solution(mesh):
    placed = (
        P("section", "dp", "mp"),
        P("section", None, None, "mp"),
        P("dp", "mp"),
        P("dp"),
        P("dp"),
    )
    return jax.shard_map(
        local, mesh=mesh, in_specs=placed, out_specs=P("section", "dp", "mp"), check_vma=False
    )
```

```python
import jax
import jax.numpy as jnp
from jax import lax
from jax.experimental import pallas as pl
from jax.experimental.pallas import tpu as pltpu
from jax.sharding import PartitionSpec as P

HS = 256
SIDE = 4
F32 = jnp.float32
BF16 = jnp.bfloat16
SWAP = [(0, 1), (1, 0)]
NT = (((1,), (1,)), ((), ()))
TN = (((0,), (0,)), ((), ()))


def shift_x(block, step):
    route = [(y * SIDE + x, y * SIDE + (x + step) % SIDE) for y in range(SIDE) for x in range(SIDE)]
    return lax.ppermute(block, "mp", route)


def shift_y(block, step):
    route = [(y * SIDE + x, (y + step) % SIDE * SIDE + x) for y in range(SIDE) for x in range(SIDE)]
    return lax.ppermute(block, "mp", route)


def cat(*parts):
    return jnp.concatenate(parts, axis=0)


def project(blocks, places, sec, own_w, other_w, total):
    rows = 3 * HS
    count = len(places)
    scalars = jnp.stack([*places, sec]).astype(jnp.int32)
    first = total is None

    def body(scalar_ref, x_ref, u_ref, r_ref, *rest):
        out_ref = rest[-1]
        step = pl.program_id(0)
        shift = pl.multiple_of(scalar_ref[count] * HS, HS)

        @pl.when(step == 0)
        def _():
            if first:
                out_ref[...] = jnp.zeros_like(out_ref)
            else:
                out_ref[...] = rest[0][...]

        low = x_ref[pl.ds(shift, HS), :]
        mid = x_ref[pl.ds(shift + HS, HS), :]
        out_ref[0] += jnp.dot(x_ref[:HS, :], u_ref[0], preferred_element_type=F32)
        out_ref[1] += jnp.dot(low, u_ref[1], preferred_element_type=F32)
        out_ref[2] += jnp.dot(mid, r_ref[0], preferred_element_type=F32)
        out_ref[3] += jnp.dot(x_ref[2 * HS :, :], r_ref[1], preferred_element_type=F32)

    whole = pl.BlockSpec((4, HS, HS), lambda i, s: (0, 0, 0))
    weight = pl.BlockSpec((2, HS, HS), lambda i, s: (0, s[i], 0))
    return pl.pallas_call(
        body,
        out_shape=jax.ShapeDtypeStruct((4, HS, HS), F32),
        grid_spec=pltpu.PrefetchScalarGridSpec(
            num_scalar_prefetch=1,
            grid=(count,),
            in_specs=[pl.BlockSpec((rows, HS), lambda i, s: (i, 0)), weight, weight] + ([] if first else [whole]),
            out_specs=whole,
        ),
        cost_estimate=pl.CostEstimate(
            flops=count * 8 * HS**3, bytes_accessed=count * 7 * HS * HS * 2, transcendentals=0
        ),
    )(scalars, blocks, own_w, other_w, *([] if first else [total]))


def attend_and_spread(total, places, sec, enc_lengths, dec_lengths, own_w, other_w):
    scale = 1.0 / HS**0.5
    count = len(places)
    scalars = jnp.stack([*places, sec, enc_lengths[sec], dec_lengths[sec]]).astype(jnp.int32)

    def body(scalar_ref, t_ref, u_ref, r_ref, out_ref, g_ref):
        @pl.when(pl.program_id(0) == 0)
        def _():
            me = scalar_ref[count]
            keys = t_ref[2 * me].astype(BF16)
            values = t_ref[2 * me + 1].astype(BF16)
            queries = t_ref[2 - 2 * me].astype(BF16)
            out_grad = t_ref[3 - 2 * me]
            live_q = lax.broadcasted_iota(jnp.int32, (HS, HS), 0) < scalar_ref[count + 2]
            live_k = lax.broadcasted_iota(jnp.int32, (HS, HS), 1) < scalar_ref[count + 1]
            masked = jnp.where(live_q, out_grad, 0.0).astype(BF16)
            scores = lax.dot_general(queries, keys, NT, preferred_element_type=F32) * scale
            scores = jnp.where(live_k, scores, -1e30)
            top = jnp.max(scores, axis=-1, keepdims=True)
            expd = jnp.exp(scores - top)
            probs = expd / jnp.sum(expd, axis=-1, keepdims=True)
            value_grad = lax.dot_general(probs.astype(BF16), masked, TN, preferred_element_type=F32).astype(BF16)
            prob_grad = lax.dot_general(masked, values, NT, preferred_element_type=F32)
            delta = jnp.sum(probs * prob_grad, axis=-1, keepdims=True)
            sg = (probs * (prob_grad - delta)).astype(BF16)
            query_grad = (jnp.dot(sg, keys, preferred_element_type=F32) * scale).astype(BF16)
            key_grad = (lax.dot_general(sg, queries, TN, preferred_element_type=F32) * scale).astype(BF16)
            g_ref[2 * me] = key_grad
            g_ref[2 * me + 1] = value_grad
            g_ref[2 - 2 * me] = query_grad
            g_ref[3 - 2 * me] = jnp.zeros_like(query_grad)

        one_block(g_ref, u_ref, r_ref, out_ref)

    whole = pl.BlockSpec((4, HS, HS), lambda i, s: (0, 0, 0))
    weight = pl.BlockSpec((2, HS, HS), lambda i, s: (0, s[i], 0))
    return pl.pallas_call(
        body,
        out_shape=(
            jax.ShapeDtypeStruct((count, 2 * HS, HS), BF16),
            jax.ShapeDtypeStruct((4, HS, HS), BF16),
        ),
        grid_spec=pltpu.PrefetchScalarGridSpec(
            num_scalar_prefetch=1,
            grid=(count,),
            in_specs=[whole, weight, weight],
            out_specs=(pl.BlockSpec((1, 2 * HS, HS), lambda i, s: (i, 0, 0)), whole),
        ),
        cost_estimate=spread_cost(count),
    )(scalars, total, own_w, other_w)


def one_block(g_ref, u_ref, r_ref, out_ref):
    for slot, w_ref in ((0, u_ref), (1, r_ref)):
        term = lax.dot_general(g_ref[2 * slot], w_ref[0], NT, preferred_element_type=F32)
        term += lax.dot_general(g_ref[2 * slot + 1], w_ref[1], NT, preferred_element_type=F32)
        out_ref[0, slot * HS : (slot + 1) * HS, :] = term.astype(BF16)


def spread_cost(count):
    return pl.CostEstimate(flops=count * 8 * HS**3, bytes_accessed=count * 12 * HS * HS, transcendentals=HS * HS)


def spread(grads, places, own_w, other_w):
    count = len(places)

    def body(scalar_ref, g_ref, u_ref, r_ref, out_ref):
        one_block(g_ref, u_ref, r_ref, out_ref)

    weight = pl.BlockSpec((2, HS, HS), lambda i, s: (0, s[i], 0))
    return pl.pallas_call(
        body,
        out_shape=jax.ShapeDtypeStruct((count, 2 * HS, HS), BF16),
        grid_spec=pltpu.PrefetchScalarGridSpec(
            num_scalar_prefetch=1,
            grid=(count,),
            in_specs=[pl.BlockSpec((4, HS, HS), lambda i, s: (0, 0, 0)), weight, weight],
            out_specs=pl.BlockSpec((1, 2 * HS, HS), lambda i, s: (i, 0, 0)),
        ),
        cost_estimate=spread_cost(count),
    )(jnp.stack(places).astype(jnp.int32), grads, own_w, other_w)


def plus(*parts):
    return sum(p.astype(F32) for p in parts).astype(BF16)


def local(states, proj_weights, out_cotangent, enc_lengths, dec_lengths):
    sec = lax.axis_index("section")
    me = lax.axis_index("mp")
    my_y, my_x = me // SIDE, me % SIDE

    def place(dy, dx):
        return (my_y + dy) % SIDE * SIDE + (my_x + dx) % SIDE

    own_w = proj_weights[0]
    rows = states[0].reshape(2, HS, HS)
    mine = lax.dynamic_index_in_dim(rows, sec, 0, keepdims=False)
    partner = lax.ppermute(lax.dynamic_index_in_dim(rows, 1 - sec, 0, keepdims=False), "section", SWAP)
    other_w = lax.ppermute(own_w, "section", SWAP)
    cotangent = lax.dynamic_slice_in_dim(out_cotangent, sec * HS, HS, 0)
    is_first = sec == 0
    c0 = cat(mine, jnp.where(is_first, partner, cotangent), jnp.where(is_first, cotangent, partner))
    n = c0.shape[0]
    h = n // 2

    up1, down1 = shift_y(c0, 1), shift_y(c0, -1)
    right0, left0, across0 = shift_x(c0, 1), shift_x(c0, -1), shift_x(c0, 2)
    pair = cat(up1, down1)
    right1, left1 = shift_x(pair, 1), shift_x(pair, -1)
    up2, down2 = shift_y(up1[:h], 1), shift_y(down1[h:], -1)
    total = project(
        cat(c0, pair, right0, left0, across0),
        [place(0, 0), place(-1, 0), place(1, 0), place(0, -1), place(0, 1), place(0, 2)],
        sec, own_w, other_w, None,
    )
    right1, left1, up2, down2, total = lax.optimization_barrier((right1, left1, up2, down2, total))
    last = cat(up2, down2)
    right2 = shift_x(cat(right1[:h], right1[n : n + h], last), 1)
    left2 = shift_x(cat(left1[h:n], left1[n + h :], last), -1)
    across2 = shift_x(last, 2)
    total = project(
        cat(right1, left1, last),
        [place(-1, -1), place(1, -1), place(-1, 1), place(1, 1), place(2, 0)],
        sec, own_w, other_w, total,
    )
    right2, left2, across2, total = lax.optimization_barrier((right2, left2, across2, total))
    total = project(
        cat(right2[:h], left2[:h], right2[h:n], left2[h:n], right2[n:], left2[n:], across2),
        [place(-1, 2), place(1, 2), place(2, -1), place(2, 1), place(2, 2)],
        sec, own_w, other_w, total,
    )

    n, h = 2 * HS, HS
    early = [(2, 1), (2, -1), (2, 2), (1, 2), (-1, 2)]
    late = [(1, 1), (1, -1), (-1, 1), (-1, -1), (0, 2), (2, 0), (1, 0), (-1, 0), (0, 1), (0, -1), (0, 0)]
    terms, grads = attend_and_spread(
        total, [place(*p) for p in early], sec, enc_lengths, dec_lengths, own_w, other_w
    )
    t = {p: terms[i] for i, p in enumerate(early)}
    right_a = shift_x(cat(t[2, 1], t[1, 2][:h], t[-1, 2][:h]), 1)
    left_a = shift_x(cat(t[2, -1], t[1, 2][h:], t[-1, 2][h:]), -1)
    across_a = shift_x(t[2, 2], 2)
    terms = spread(grads, [place(*p) for p in late], own_w, other_w)
    t |= {p: terms[i] for i, p in enumerate(late)}

    far = plus(t[2, 0], right_a[:n], left_a[:n], across_a)
    up_b, down_b = shift_y(far[:h], 1), shift_y(far[h:], -1)
    right_b = shift_x(
        cat(
            plus(t[1, 1][:h], right_a[n : n + h]), t[1, 1][h:],
            plus(t[-1, 1][:h], right_a[n + h :]), t[-1, 1][h:],
            t[0, 2][:h],
        ),
        1,
    )
    left_b = shift_x(
        cat(
            t[1, -1][:h], plus(t[1, -1][h:], left_a[n : n + h]),
            t[-1, -1][:h], plus(t[-1, -1][h:], left_a[n + h :]),
            t[0, 2][h:],
        ),
        -1,
    )
    up_c = shift_y(
        cat(
            plus(t[1, 0][:h], right_b[:h], left_b[:h], up_b),
            plus(t[1, 0][h:], right_b[h:n], left_b[h:n]),
        ),
        1,
    )
    down_c = shift_y(
        cat(
            plus(t[-1, 0][:h], right_b[n : n + h], left_b[n : n + h]),
            plus(t[-1, 0][h:], right_b[n + h : 2 * n], left_b[n + h : 2 * n], down_b),
        ),
        -1,
    )
    right_c = shift_x(cat(plus(t[0, 1][:h], right_b[2 * n :]), t[0, 1][h:]), 1)
    left_c = shift_x(cat(t[0, -1][:h], plus(t[0, -1][h:], left_b[2 * n :])), -1)
    swapped = lax.ppermute(plus(t[0, 0][h:], right_c[h:], left_c[h:], up_c[h:], down_c[h:]), "section", SWAP)
    kept = plus(t[0, 0][:h], right_c[:h], left_c[:h], up_c[:h], down_c[:h])
    return jnp.where(is_first, cat(kept, swapped), cat(swapped, kept))[None]


def solution(mesh):
    placed = (
        P("section", "dp", "mp"),
        P("section", None, None, "mp"),
        P("dp", "mp"),
        P("dp"),
        P("dp"),
    )
    return jax.shard_map(
        local, mesh=mesh, in_specs=placed, out_specs=P("section", "dp", "mp"), check_vma=False
    )
```

```python
import jax
import jax.numpy as jnp
from jax import lax
from jax.experimental import pallas as pl
from jax.experimental.pallas import tpu as pltpu
from jax.sharding import PartitionSpec as P

HS = 256
SIDE = 4
ROWS = 3 * HS
HALF = ROWS // 2
N = 2 * HS
F32 = jnp.float32
BF16 = jnp.bfloat16
SWAP = [(0, 1), (1, 0)]
NT = (((1,), (1,)), ((), ()))
TN = (((0,), (0,)), ((), ()))
VMEM = pl.BlockSpec(memory_space=pltpu.VMEM)
SMEM = pl.BlockSpec(memory_space=pltpu.SMEM)


def shift_x(block, step):
    route = [(y * SIDE + x, y * SIDE + (x + step) % SIDE) for y in range(SIDE) for x in range(SIDE)]
    return lax.ppermute(block, "mp", route)


def shift_y(block, step):
    route = [(y * SIDE + x, (y + step) % SIDE * SIDE + x) for y in range(SIDE) for x in range(SIDE)]
    return lax.ppermute(block, "mp", route)


def call(body, inputs, rows, flops=0, out_dtype=BF16, shapes=None):
    shapes = shapes or [(r, HS) for r in rows]
    out = [jax.ShapeDtypeStruct(s, out_dtype) for s in shapes]
    moved = sum(a.size * a.dtype.itemsize for a in inputs[1:])
    return pl.pallas_call(
        body,
        out_shape=out,
        in_specs=[SMEM] + [VMEM] * (len(inputs) - 1),
        out_specs=[VMEM] * len(out),
        cost_estimate=pl.CostEstimate(flops=flops, bytes_accessed=moved, transcendentals=0),
    )(*inputs)


def assemble(table, own, cotangent, partner):
    def body(table_ref, own_ref, cot_ref, partner_ref, out_ref):
        sec = table_ref[0]
        here = pl.ds(pl.multiple_of(sec * HS, HS), HS)
        out_ref[:HS, :] = own_ref[here, :]
        out_ref[pl.ds(pl.multiple_of((2 - sec) * HS, HS), HS), :] = cot_ref[here, :]
        out_ref[pl.ds(pl.multiple_of((1 + sec) * HS, HS), HS), :] = partner_ref[here, :]

    return call(body, [table, own, cotangent, partner], [ROWS])[0]


def rows_of(refs, block, low, high):
    parts, at = [], 0
    for which, first, count in block:
        a, b = max(low, at), min(high, at + count)
        if a < b:
            parts.append(refs[which][first + a - at : first + b - at, :])
        at += count
    return parts[0] if len(parts) == 1 else jnp.concatenate(parts, axis=0)


def project(table, pieces, blocks, own_w, other_w, total):
    def body(table_ref, u_ref, r_ref, *rest):
        refs, out_ref = rest[: len(pieces)], rest[-1]
        core0 = table_ref[0] == 0
        sums = [None if total is None else rest[-2][j] for j in range(4)]
        for entry, block in blocks:
            feats = pl.ds(pl.multiple_of(table_ref[entry] * HS, HS), HS)
            p0 = rows_of(refs, block, 0, HS)
            p1 = rows_of(refs, block, HS, 2 * HS)
            p2 = rows_of(refs, block, 2 * HS, 3 * HS)
            for j, (rows, weight) in enumerate((
                (p0, u_ref[0, feats, :]),
                (jnp.where(core0, p0, p1), u_ref[1, feats, :]),
                (jnp.where(core0, p1, p2), r_ref[0, feats, :]),
                (p2, r_ref[1, feats, :]),
            )):
                term = jnp.dot(rows, weight, preferred_element_type=F32)
                sums[j] = term if sums[j] is None else sums[j] + term
        for j in range(4):
            out_ref[j] = sums[j]

    inputs = [table, own_w, other_w, *pieces] + ([] if total is None else [total])
    flops = len(blocks) * 8 * HS**3
    return call(body, inputs, None, flops, F32, [(4, HS, HS)])[0]


def term_of(g_ref, u_ref, r_ref, index, slot):
    w_ref = (u_ref, r_ref)[slot]
    feats = pl.ds(pl.multiple_of(index * HS, HS), HS)
    term = lax.dot_general(g_ref[2 * slot], w_ref[0, feats, :], NT, preferred_element_type=F32)
    term += lax.dot_general(g_ref[2 * slot + 1], w_ref[1, feats, :], NT, preferred_element_type=F32)
    return term.astype(BF16)


def write_terms(table_ref, g_ref, u_ref, r_ref, wanted):
    for entry, *slots in wanted:
        for slot, (out_ref, row) in enumerate(slots):
            out_ref[row : row + HS, :] = term_of(g_ref, u_ref, r_ref, table_ref[entry], slot)


def attend(table, total, own_w, other_w, at):
    scale = 1.0 / HS**0.5

    def body(table_ref, t_ref, u_ref, r_ref, right_ref, left_ref, across_ref, g_ref):
        me = table_ref[0]
        keys = t_ref[2 * me].astype(BF16)
        values = t_ref[2 * me + 1].astype(BF16)
        queries = t_ref[2 - 2 * me].astype(BF16)
        out_grad = t_ref[3 - 2 * me]
        live_q = lax.broadcasted_iota(jnp.int32, (HS, HS), 0) < table_ref[2]
        live_k = lax.broadcasted_iota(jnp.int32, (HS, HS), 1) < table_ref[1]
        masked = jnp.where(live_q, out_grad, 0.0).astype(BF16)
        scores = lax.dot_general(queries, keys, NT, preferred_element_type=F32) * scale
        scores = jnp.where(live_k, scores, -1e30)
        top = jnp.max(scores, axis=-1, keepdims=True)
        expd = jnp.exp(scores - top)
        probs = expd / jnp.sum(expd, axis=-1, keepdims=True)
        value_grad = lax.dot_general(probs.astype(BF16), masked, TN, preferred_element_type=F32).astype(BF16)
        prob_grad = lax.dot_general(masked, values, NT, preferred_element_type=F32)
        delta = jnp.sum(probs * prob_grad, axis=-1, keepdims=True)
        sg = (probs * (prob_grad - delta)).astype(BF16)
        query_grad = (jnp.dot(sg, keys, preferred_element_type=F32) * scale).astype(BF16)
        key_grad = (lax.dot_general(sg, queries, TN, preferred_element_type=F32) * scale).astype(BF16)
        g_ref[2 * me] = key_grad
        g_ref[2 * me + 1] = value_grad
        g_ref[2 - 2 * me] = query_grad
        g_ref[3 - 2 * me] = jnp.zeros_like(query_grad)
        write_terms(table_ref, g_ref, u_ref, r_ref, [
            (at[2, 1], (right_ref, 0), (right_ref, HS)),
            (at[1, 2], (right_ref, N), (left_ref, N)),
            (at[-1, 2], (right_ref, N + HS), (left_ref, N + HS)),
            (at[2, -1], (left_ref, 0), (left_ref, HS)),
            (at[2, 2], (across_ref, 0), (across_ref, HS)),
        ])

    shapes = [(2 * N, HS), (2 * N, HS), (N, HS), (4, HS, HS)]
    return call(body, [table, total, own_w, other_w], None, 60 * HS**3, BF16, shapes)


def spread(table, grads, own_w, other_w, at):
    def body(table_ref, g_ref, u_ref, r_ref, far, right, left, up, down, right_c, left_c, here):
        write_terms(table_ref, g_ref, u_ref, r_ref, [
            (at[2, 0], (far, 0), (far, HS)),
            (at[1, 1], (right, 0), (right, HS)),
            (at[-1, 1], (right, N), (right, N + HS)),
            (at[1, -1], (left, 0), (left, HS)),
            (at[-1, -1], (left, N), (left, N + HS)),
            (at[0, 2], (right, 2 * N), (left, 2 * N)),
            (at[1, 0], (up, 0), (up, HS)),
            (at[-1, 0], (down, 0), (down, HS)),
            (at[0, 1], (right_c, 0), (right_c, HS)),
            (at[0, -1], (left_c, 0), (left_c, HS)),
            (at[0, 0], (here, 0), (here, HS)),
        ])

    rows = [N, 2 * N + HS, 2 * N + HS, N, N, N, N, N]
    return call(body, [table, grads, own_w, other_w], rows, 88 * HS**3)


def add_rows(table, sources, rows, recipe):
    def body(table_ref, *refs):
        ins, outs = refs[: len(sources)], refs[len(sources) :]
        for out, row, parts in recipe:
            value = ins[parts[0][0]][parts[0][1] : parts[0][1] + HS, :]
            if len(parts) > 1:
                value = value.astype(F32)
                for source, first in parts[1:]:
                    value += ins[source][first : first + HS, :].astype(F32)
            outs[out][row : row + HS, :] = value.astype(BF16)

    return call(body, [table, *sources], rows)


def local(states, proj_weights, out_cotangent, enc_lengths, dec_lengths):
    sec = lax.axis_index("section")
    me = lax.axis_index("mp")
    my_y, my_x = me // SIDE, me % SIDE
    offsets = [(dy, dx) for dy in (0, 1, 2, -1) for dx in (0, 1, 2, -1)]
    at = {offset: 3 + i for i, offset in enumerate(offsets)}
    dy, dx = (jnp.array(v, jnp.int32) for v in zip(*offsets, strict=True))
    places = (my_y + dy) % SIDE * SIDE + (my_x + dx) % SIDE
    lengths = jnp.stack([enc_lengths, dec_lengths], axis=1)[sec]
    table = jnp.concatenate([sec[None], lengths, places]).astype(jnp.int32)

    own = states[0]
    partner = lax.ppermute(own, "section", SWAP)
    own_w, partner = lax.optimization_barrier((proj_weights[0], partner))
    other_w = lax.ppermute(own_w, "section", SWAP)
    c0 = assemble(table, own, out_cotangent, partner)

    up1, down1 = shift_y(c0, 1), shift_y(c0, -1)
    right0, left0, across0 = shift_x(c0, 1), shift_x(c0, -1), shift_x(c0, 2)
    c0, up1, down1, right0, left0, across0 = lax.optimization_barrier((c0, up1, down1, right0, left0, across0))

    pair = jnp.concatenate([up1, down1], axis=0)
    right1, left1 = shift_x(pair, 1), shift_x(pair, -1)
    up2, down2 = shift_y(up1[:HALF], 1), shift_y(down1[HALF:], -1)
    total = project(
        table, [c0, pair, right0, left0, across0],
        [
            (at[0, 0], [(0, 0, ROWS)]), (at[-1, 0], [(1, 0, ROWS)]), (at[1, 0], [(1, ROWS, ROWS)]),
            (at[0, -1], [(2, 0, ROWS)]), (at[0, 1], [(3, 0, ROWS)]), (at[0, 2], [(4, 0, ROWS)]),
        ],
        own_w, other_w, None,
    )
    right1, left1, up2, down2, total = lax.optimization_barrier((right1, left1, up2, down2, total))

    last = jnp.concatenate([up2, down2], axis=0)
    right2 = shift_x(jnp.concatenate([right1[:HALF], right1[ROWS : ROWS + HALF], last], axis=0), 1)
    left2 = shift_x(jnp.concatenate([left1[HALF:ROWS], left1[ROWS + HALF :], last], axis=0), -1)
    across2 = shift_x(last, 2)
    total = project(
        table, [right1, left1, last],
        [
            (at[-1, -1], [(0, 0, ROWS)]), (at[1, -1], [(0, ROWS, ROWS)]),
            (at[-1, 1], [(1, 0, ROWS)]), (at[1, 1], [(1, ROWS, ROWS)]), (at[2, 0], [(2, 0, ROWS)]),
        ],
        own_w, other_w, total,
    )
    right2, left2, across2, total = lax.optimization_barrier((right2, left2, across2, total))
    total = project(
        table, [right2, left2, across2],
        [
            (at[-1, 2], [(0, 0, HALF), (1, 0, HALF)]), (at[1, 2], [(0, HALF, HALF), (1, HALF, HALF)]),
            (at[2, -1], [(0, ROWS, ROWS)]), (at[2, 1], [(1, ROWS, ROWS)]), (at[2, 2], [(2, 0, ROWS)]),
        ],
        own_w, other_w, total,
    )

    right_a, left_a, across_a, grads = attend(table, total, own_w, other_w, at)
    right_a, left_a, across_a = shift_x(right_a, 1), shift_x(left_a, -1), shift_x(across_a, 2)
    far, right_b, left_b, up_c, down_c, right_c, left_c, here = spread(table, grads, own_w, other_w, at)
    far, right_b, left_b = add_rows(
        table, [far, right_b, left_b, right_a, left_a, across_a], [N, 2 * N + HS, 2 * N + HS],
        [
            (0, 0, [(0, 0), (3, 0), (4, 0), (5, 0)]), (0, HS, [(0, HS), (3, HS), (4, HS), (5, HS)]),
            (1, 0, [(1, 0), (3, N)]), (1, HS, [(1, HS)]),
            (1, N, [(1, N), (3, N + HS)]), (1, N + HS, [(1, N + HS)]), (1, 2 * N, [(1, 2 * N)]),
            (2, 0, [(2, 0)]), (2, HS, [(2, HS), (4, N)]),
            (2, N, [(2, N)]), (2, N + HS, [(2, N + HS), (4, N + HS)]), (2, 2 * N, [(2, 2 * N)]),
        ],
    )
    up_b, down_b = shift_y(far[:HS], 1), shift_y(far[HS:], -1)
    right_b, left_b = shift_x(right_b, 1), shift_x(left_b, -1)
    up_c, down_c, right_c, left_c = add_rows(
        table, [up_c, down_c, right_c, left_c, right_b, left_b, up_b, down_b], [N] * 4,
        [
            (0, 0, [(0, 0), (4, 0), (5, 0), (6, 0)]), (0, HS, [(0, HS), (4, HS), (5, HS)]),
            (1, 0, [(1, 0), (4, N), (5, N)]), (1, HS, [(1, HS), (4, N + HS), (5, N + HS), (7, 0)]),
            (2, 0, [(2, 0), (4, 2 * N)]), (2, HS, [(2, HS)]),
            (3, 0, [(3, 0)]), (3, HS, [(3, HS), (5, 2 * N)]),
        ],
    )
    up_c, down_c, right_c, left_c = shift_y(up_c, 1), shift_y(down_c, -1), shift_x(right_c, 1), shift_x(left_c, -1)
    kept, sent = add_rows(
        table, [here, up_c, down_c, right_c, left_c], [HS, HS],
        [(0, 0, [(i, 0) for i in range(5)]), (1, 0, [(i, HS) for i in range(5)])],
    )
    swapped = lax.ppermute(sent, "section", SWAP)
    first = sec == 0
    return jnp.where(first, jnp.concatenate([kept, swapped]), jnp.concatenate([swapped, kept]))[None]


def solution(mesh):
    placed = (
        P("section", "dp", "mp"),
        P("section", None, None, "mp"),
        P("dp", "mp"),
        P("dp"),
        P("dp"),
    )
    return jax.shard_map(
        local, mesh=mesh, in_specs=placed, out_specs=P("section", "dp", "mp"), check_vma=False
    )
```

```python
import jax
import jax.numpy as jnp
from jax import lax
from jax.experimental import pallas as pl
from jax.experimental.pallas import tpu as pltpu
from jax.sharding import PartitionSpec as P

HS = 256
SIDE = 4
ROWS = 3 * HS
HALF = ROWS // 2
N = 2 * HS
F32 = jnp.float32
BF16 = jnp.bfloat16
SWAP = [(0, 1), (1, 0)]
NT = (((1,), (1,)), ((), ()))
TN = (((0,), (0,)), ((), ()))
VMEM = pl.BlockSpec(memory_space=pltpu.VMEM)
SMEM = pl.BlockSpec(memory_space=pltpu.SMEM)
VMEM_LIMIT = 20 * 2**20


def shift_x(block, step):
    route = [(y * SIDE + x, y * SIDE + (x + step) % SIDE) for y in range(SIDE) for x in range(SIDE)]
    return lax.ppermute(block, "mp", route)


def shift_y(block, step):
    route = [(y * SIDE + x, (y + step) % SIDE * SIDE + x) for y in range(SIDE) for x in range(SIDE)]
    return lax.ppermute(block, "mp", route)


def call(body, inputs, shapes, flops=0, out_dtype=BF16, scalars=0):
    out = [jax.ShapeDtypeStruct(s, out_dtype) for s in shapes]
    moved = sum(a.size * a.dtype.itemsize for a in inputs)
    return pl.pallas_call(
        body,
        out_shape=out,
        in_specs=[SMEM] * scalars + [VMEM] * (len(inputs) - scalars),
        out_specs=[VMEM] * len(out),
        compiler_params=pltpu.CompilerParams(vmem_limit_bytes=VMEM_LIMIT),
        cost_estimate=pl.CostEstimate(flops=flops, bytes_accessed=moved, transcendentals=0),
    )(*inputs)


def feature_rows(offset):
    me = lax.axis_index("mp")
    y = lax.rem(lax.div(me, SIDE) + offset[0] + SIDE, SIDE)
    x = lax.rem(lax.rem(me, SIDE) + offset[1] + SIDE, SIDE)
    return pl.ds(pl.multiple_of((y * SIDE + x) * HS, HS), HS)


def slot_rows(index):
    return pl.ds(pl.multiple_of(index * HS, HS), HS)


def assemble(own, cotangent, partner):
    def body(own_ref, cot_ref, partner_ref, out_ref):
        sec = lax.axis_index("section")
        here = slot_rows(sec)
        out_ref[:HS, :] = own_ref[here, :]
        out_ref[slot_rows(2 - sec), :] = cot_ref[here, :]
        out_ref[slot_rows(1 + sec), :] = partner_ref[here, :]

    return call(body, [own, cotangent, partner], [(ROWS, HS)])[0]


def rows_of(refs, block, low, high):
    parts, at = [], 0
    for which, first, count in block:
        a, b = max(low, at), min(high, at + count)
        if a < b:
            parts.append(refs[which][first + a - at : first + b - at, :])
        at += count
    return parts[0] if len(parts) == 1 else jnp.concatenate(parts, axis=0)


def project(pieces, blocks, own_w, other_w, total):
    def body(u_ref, r_ref, *rest):
        refs, out_ref = rest[: len(pieces)], rest[-1]
        core0 = lax.axis_index("section") == 0
        feats = [feature_rows(offset) for offset, _ in blocks]
        parts = [
            jnp.concatenate([rows_of(refs, block, k * HS, (k + 1) * HS) for _, block in blocks], axis=1)
            for k in range(3)
        ]
        lhs = (parts[0], jnp.where(core0, parts[0], parts[1]), jnp.where(core0, parts[1], parts[2]), parts[2])
        for j in range(4):
            w_ref = (u_ref, r_ref)[j // 2]
            weight = jnp.concatenate([w_ref[j % 2, f, :] for f in feats], axis=0)
            term = jnp.dot(lhs[j], weight, preferred_element_type=F32)
            out_ref[j] = term if total is None else rest[-2][j] + term

    inputs = [own_w, other_w, *pieces] + ([] if total is None else [total])
    return call(body, inputs, [(4, HS, HS)], len(blocks) * 8 * HS**3, F32)[0]


def write_terms(g_ref, u_ref, r_ref, wanted):
    for offset, *slots in wanted:
        feats = feature_rows(offset)
        for slot, (out_ref, row) in enumerate(slots):
            w_ref = (u_ref, r_ref)[slot]
            term = lax.dot_general(g_ref[2 * slot], w_ref[0, feats, :], NT, preferred_element_type=F32)
            term += lax.dot_general(g_ref[2 * slot + 1], w_ref[1, feats, :], NT, preferred_element_type=F32)
            out_ref[row : row + HS, :] = term.astype(BF16)


def attend(enc_lengths, dec_lengths, total, own_w, other_w):
    scale = 1.0 / HS**0.5

    def body(enc_ref, dec_ref, t_ref, u_ref, r_ref, right_ref, left_ref, across_ref, g_ref):
        me = lax.axis_index("section")
        keys = t_ref[2 * me].astype(BF16)
        values = t_ref[2 * me + 1].astype(BF16)
        queries = t_ref[2 - 2 * me].astype(BF16)
        out_grad = t_ref[3 - 2 * me]
        live_q = lax.broadcasted_iota(jnp.int32, (HS, HS), 0) < dec_ref[me]
        live_k = lax.broadcasted_iota(jnp.int32, (HS, HS), 1) < enc_ref[me]
        masked = jnp.where(live_q, out_grad, 0.0).astype(BF16)
        scores = lax.dot_general(queries, keys, NT, preferred_element_type=F32) * scale
        scores = jnp.where(live_k, scores, -1e30)
        top = jnp.max(scores, axis=-1, keepdims=True)
        expd = jnp.exp(scores - top)
        probs = expd / jnp.sum(expd, axis=-1, keepdims=True)
        value_grad = lax.dot_general(probs.astype(BF16), masked, TN, preferred_element_type=F32).astype(BF16)
        prob_grad = lax.dot_general(masked, values, NT, preferred_element_type=F32)
        delta = jnp.sum(probs * prob_grad, axis=-1, keepdims=True)
        sg = (probs * (prob_grad - delta)).astype(BF16)
        query_grad = (jnp.dot(sg, keys, preferred_element_type=F32) * scale).astype(BF16)
        key_grad = (lax.dot_general(sg, queries, TN, preferred_element_type=F32) * scale).astype(BF16)
        g_ref[2 * me] = key_grad
        g_ref[2 * me + 1] = value_grad
        g_ref[2 - 2 * me] = query_grad
        g_ref[3 - 2 * me] = jnp.zeros_like(query_grad)
        write_terms(g_ref, u_ref, r_ref, [
            ((2, 1), (right_ref, 0), (right_ref, HS)),
            ((1, 2), (right_ref, N), (left_ref, N)),
            ((-1, 2), (right_ref, N + HS), (left_ref, N + HS)),
            ((2, -1), (left_ref, 0), (left_ref, HS)),
            ((2, 2), (across_ref, 0), (across_ref, HS)),
        ])

    shapes = [(2 * N, HS), (2 * N, HS), (N, HS), (4, HS, HS)]
    return call(body, [enc_lengths, dec_lengths, total, own_w, other_w], shapes, 60 * HS**3, BF16, 2)


def spread(grads, own_w, other_w):
    def body(g_ref, u_ref, r_ref, far, right, left, up, down, right_c, left_c, here):
        write_terms(g_ref, u_ref, r_ref, [
            ((2, 0), (far, 0), (far, HS)),
            ((1, 1), (right, 0), (right, HS)),
            ((-1, 1), (right, N), (right, N + HS)),
            ((1, -1), (left, 0), (left, HS)),
            ((-1, -1), (left, N), (left, N + HS)),
            ((0, 2), (right, 2 * N), (left, 2 * N)),
            ((1, 0), (up, 0), (up, HS)),
            ((-1, 0), (down, 0), (down, HS)),
            ((0, 1), (right_c, 0), (right_c, HS)),
            ((0, -1), (left_c, 0), (left_c, HS)),
            ((0, 0), (here, 0), (here, HS)),
        ])

    rows = [N, 2 * N + HS, 2 * N + HS, N, N, N, N, N]
    return call(body, [grads, own_w, other_w], [(r, HS) for r in rows], 88 * HS**3)


def add_rows(sources, rows, recipe):
    def body(*refs):
        ins, outs = refs[: len(sources)], refs[len(sources) :]
        for out, row, parts in recipe:
            value = ins[parts[0][0]][parts[0][1] : parts[0][1] + HS, :]
            if len(parts) > 1:
                value = value.astype(F32)
                for source, first in parts[1:]:
                    value += ins[source][first : first + HS, :].astype(F32)
            outs[out][row : row + HS, :] = value.astype(BF16)

    return call(body, list(sources), [(r, HS) for r in rows])


def finish(here, arrived, swapped):
    def body(here_ref, *rest):
        sec = lax.axis_index("section")
        value = here_ref[:HS, :].astype(F32)
        for ref in rest[:4]:
            value += ref[:HS, :].astype(F32)
        rest[-1][slot_rows(sec), :] = value.astype(BF16)
        rest[-1][slot_rows(1 - sec), :] = rest[4][...]

    return call(body, [here, *arrived, swapped], [(N, HS)])[0]


def local(states, proj_weights, out_cotangent, enc_lengths, dec_lengths):
    own = states[0]
    partner = lax.ppermute(own, "section", SWAP)
    c0 = assemble(own, out_cotangent, partner)

    up1, down1 = shift_y(c0, 1), shift_y(c0, -1)
    right0, left0, across0 = shift_x(c0, 1), shift_x(c0, -1), shift_x(c0, 2)
    own_w, right0 = lax.optimization_barrier((proj_weights[0], right0))
    other_w = lax.ppermute(own_w, "section", SWAP)
    c0, up1, down1, right0, left0, across0 = lax.optimization_barrier((c0, up1, down1, right0, left0, across0))

    pair = jnp.concatenate([up1, down1], axis=0)
    right1, left1 = shift_x(pair, 1), shift_x(pair, -1)
    up2, down2 = shift_y(up1[:HALF], 1), shift_y(down1[HALF:], -1)
    total = project(
        [c0, pair, right0, left0, across0],
        [
            ((0, 0), [(0, 0, ROWS)]), ((-1, 0), [(1, 0, ROWS)]), ((1, 0), [(1, ROWS, ROWS)]),
            ((0, -1), [(2, 0, ROWS)]), ((0, 1), [(3, 0, ROWS)]), ((0, 2), [(4, 0, ROWS)]),
        ],
        own_w, other_w, None,
    )
    right1, left1, up2, down2, total = lax.optimization_barrier((right1, left1, up2, down2, total))

    last = jnp.concatenate([up2, down2], axis=0)
    right2 = shift_x(jnp.concatenate([right1[:HALF], right1[ROWS : ROWS + HALF], last], axis=0), 1)
    left2 = shift_x(jnp.concatenate([left1[HALF:ROWS], left1[ROWS + HALF :], last], axis=0), -1)
    across2 = shift_x(last, 2)
    total = project(
        [right1, left1, last],
        [
            ((-1, -1), [(0, 0, ROWS)]), ((1, -1), [(0, ROWS, ROWS)]),
            ((-1, 1), [(1, 0, ROWS)]), ((1, 1), [(1, ROWS, ROWS)]), ((2, 0), [(2, 0, ROWS)]),
        ],
        own_w, other_w, total,
    )
    right2, left2, across2, total = lax.optimization_barrier((right2, left2, across2, total))
    total = project(
        [right2, left2, across2],
        [
            ((-1, 2), [(0, 0, HALF), (1, 0, HALF)]), ((1, 2), [(0, HALF, HALF), (1, HALF, HALF)]),
            ((2, -1), [(0, ROWS, ROWS)]), ((2, 1), [(1, ROWS, ROWS)]), ((2, 2), [(2, 0, ROWS)]),
        ],
        own_w, other_w, total,
    )

    right_a, left_a, across_a, grads = attend(enc_lengths, dec_lengths, total, own_w, other_w)
    right_a, left_a, across_a = shift_x(right_a, 1), shift_x(left_a, -1), shift_x(across_a, 2)
    far, right_b, left_b, up_c, down_c, right_c, left_c, here = spread(grads, own_w, other_w)
    far, right_b, left_b = add_rows(
        [far, right_b, left_b, right_a, left_a, across_a], [N, 2 * N + HS, 2 * N + HS],
        [
            (0, 0, [(0, 0), (3, 0), (4, 0), (5, 0)]), (0, HS, [(0, HS), (3, HS), (4, HS), (5, HS)]),
            (1, 0, [(1, 0), (3, N)]), (1, HS, [(1, HS)]),
            (1, N, [(1, N), (3, N + HS)]), (1, N + HS, [(1, N + HS)]), (1, 2 * N, [(1, 2 * N)]),
            (2, 0, [(2, 0)]), (2, HS, [(2, HS), (4, N)]),
            (2, N, [(2, N)]), (2, N + HS, [(2, N + HS), (4, N + HS)]), (2, 2 * N, [(2, 2 * N)]),
        ],
    )
    up_b, down_b = shift_y(far[:HS], 1), shift_y(far[HS:], -1)
    right_b, left_b = shift_x(right_b, 1), shift_x(left_b, -1)
    up_c, down_c, right_c, left_c = add_rows(
        [up_c, down_c, right_c, left_c, right_b, left_b, up_b, down_b], [N] * 4,
        [
            (0, 0, [(0, 0), (4, 0), (5, 0), (6, 0)]), (0, HS, [(0, HS), (4, HS), (5, HS)]),
            (1, 0, [(1, 0), (4, N), (5, N)]), (1, HS, [(1, HS), (4, N + HS), (5, N + HS), (7, 0)]),
            (2, 0, [(2, 0), (4, 2 * N)]), (2, HS, [(2, HS)]),
            (3, 0, [(3, 0)]), (3, HS, [(3, HS), (5, 2 * N)]),
        ],
    )
    up_c, down_c, right_c, left_c = shift_y(up_c, 1), shift_y(down_c, -1), shift_x(right_c, 1), shift_x(left_c, -1)
    arrived = [up_c, down_c, right_c, left_c]
    sent = add_rows([here, *arrived], [HS], [(0, 0, [(i, HS) for i in range(5)])])[0]
    swapped = lax.ppermute(sent, "section", SWAP)
    return finish(here, arrived, swapped)[None]


def solution(mesh):
    placed = (
        P("section", "dp", "mp"),
        P("section", None, None, "mp"),
        P("dp", "mp"),
        P("dp"),
        P("dp"),
    )
    return jax.shard_map(
        local, mesh=mesh, in_specs=placed, out_specs=P("section", "dp", "mp"), check_vma=False
    )
```

```python
import jax
import jax.numpy as jnp
from jax import lax
from jax.experimental import pallas as pl
from jax.experimental.pallas import tpu as pltpu
from jax.sharding import PartitionSpec as P

HS = 256
SIDE = 4
ROWS = 3 * HS
HALF = ROWS // 2
N = 2 * HS
F32 = jnp.float32
BF16 = jnp.bfloat16
SWAP = [(0, 1), (1, 0)]
NT = (((1,), (1,)), ((), ()))
TN = (((0,), (0,)), ((), ()))
VMEM = pl.BlockSpec(memory_space=pltpu.VMEM)
SMEM = pl.BlockSpec(memory_space=pltpu.SMEM)
VMEM_LIMIT = 20 * 2**20


def shift_x(block, step):
    route = [(y * SIDE + x, y * SIDE + (x + step) % SIDE) for y in range(SIDE) for x in range(SIDE)]
    return lax.ppermute(block, "mp", route)


def shift_y(block, step):
    route = [(y * SIDE + x, (y + step) % SIDE * SIDE + x) for y in range(SIDE) for x in range(SIDE)]
    return lax.ppermute(block, "mp", route)


def call(body, inputs, shapes, flops=0, out_dtype=BF16, scalars=0):
    out = [jax.ShapeDtypeStruct(s, out_dtype) for s in shapes]
    moved = sum(a.size * a.dtype.itemsize for a in inputs)
    return pl.pallas_call(
        body,
        out_shape=out,
        in_specs=[SMEM] * scalars + [VMEM] * (len(inputs) - scalars),
        out_specs=[VMEM] * len(out),
        compiler_params=pltpu.CompilerParams(vmem_limit_bytes=VMEM_LIMIT),
        cost_estimate=pl.CostEstimate(flops=flops, bytes_accessed=moved, transcendentals=0),
    )(*inputs)


def feature_rows(offset):
    me = lax.axis_index("mp")
    y = lax.rem(lax.div(me, SIDE) + offset[0] + SIDE, SIDE)
    x = lax.rem(lax.rem(me, SIDE) + offset[1] + SIDE, SIDE)
    return pl.ds(pl.multiple_of((y * SIDE + x) * HS, HS), HS)


def slot_rows(index):
    return pl.ds(pl.multiple_of(index * HS, HS), HS)


def assemble(own, cotangent, partner):
    def body(own_ref, cot_ref, partner_ref, out_ref):
        sec = lax.axis_index("section")
        here = slot_rows(sec)
        out_ref[:HS, :] = own_ref[here, :]
        out_ref[slot_rows(2 - sec), :] = cot_ref[here, :]
        out_ref[slot_rows(1 + sec), :] = partner_ref[here, :]

    return call(body, [own, cotangent, partner], [(ROWS, HS)])[0]


def rows_of(refs, block, low, high):
    parts, at = [], 0
    for which, first, count in block:
        a, b = max(low, at), min(high, at + count)
        if a < b:
            parts.append(refs[which][first + a - at : first + b - at, :])
        at += count
    return parts[0] if len(parts) == 1 else jnp.concatenate(parts, axis=0)


def project(pieces, blocks, own_w, other_w, total):
    def body(u_ref, r_ref, *rest):
        refs, out_ref = rest[: len(pieces)], rest[-1]
        core0 = lax.axis_index("section") == 0
        feats = [feature_rows(offset) for offset, _ in blocks]
        parts = [
            jnp.concatenate([rows_of(refs, block, k * HS, (k + 1) * HS) for _, block in blocks], axis=1)
            for k in range(3)
        ]
        lhs = (parts[0], jnp.where(core0, parts[0], parts[1]), jnp.where(core0, parts[1], parts[2]), parts[2])
        for j in range(4):
            w_ref = (u_ref, r_ref)[j // 2]
            weight = jnp.concatenate([w_ref[j % 2, f, :] for f in feats], axis=0)
            term = jnp.dot(lhs[j], weight, preferred_element_type=F32)
            out_ref[j] = term if total is None else rest[-2][j] + term

    inputs = [own_w, other_w, *pieces] + ([] if total is None else [total])
    return call(body, inputs, [(4, HS, HS)], len(blocks) * 8 * HS**3, F32)[0]


def write_terms(g_ref, u_ref, r_ref, wanted):
    for offset, *slots in wanted:
        feats = feature_rows(offset)
        for slot, (out_ref, row) in enumerate(slots):
            w_ref = (u_ref, r_ref)[slot]
            term = lax.dot_general(g_ref[2 * slot], w_ref[0, feats, :], NT, preferred_element_type=F32)
            term += lax.dot_general(g_ref[2 * slot + 1], w_ref[1, feats, :], NT, preferred_element_type=F32)
            out_ref[row : row + HS, :] = term.astype(BF16)


def attend(enc_lengths, dec_lengths, total, own_w, other_w):
    scale = 1.0 / HS**0.5

    def body(enc_ref, dec_ref, t_ref, u_ref, r_ref, right_ref, left_ref, across_ref, g_ref):
        me = lax.axis_index("section")
        keys = t_ref[2 * me].astype(BF16)
        values = t_ref[2 * me + 1].astype(BF16)
        queries = t_ref[2 - 2 * me].astype(BF16)
        out_grad = t_ref[3 - 2 * me]
        live_q = lax.broadcasted_iota(jnp.int32, (HS, HS), 0) < dec_ref[me]
        live_k = lax.broadcasted_iota(jnp.int32, (HS, HS), 1) < enc_ref[me]
        masked = jnp.where(live_q, out_grad, 0.0).astype(BF16)
        scores = lax.dot_general(queries, keys, NT, preferred_element_type=F32) * scale
        scores = jnp.where(live_k, scores, -1e30)
        top = jnp.max(scores, axis=-1, keepdims=True)
        expd = jnp.exp(scores - top)
        probs = expd / jnp.sum(expd, axis=-1, keepdims=True)
        value_grad = lax.dot_general(probs.astype(BF16), masked, TN, preferred_element_type=F32).astype(BF16)
        prob_grad = lax.dot_general(masked, values, NT, preferred_element_type=F32)
        delta = jnp.sum(probs * prob_grad, axis=-1, keepdims=True)
        sg = (probs * (prob_grad - delta)).astype(BF16)
        query_grad = (jnp.dot(sg, keys, preferred_element_type=F32) * scale).astype(BF16)
        key_grad = (lax.dot_general(sg, queries, TN, preferred_element_type=F32) * scale).astype(BF16)
        g_ref[2 * me] = key_grad
        g_ref[2 * me + 1] = value_grad
        g_ref[2 - 2 * me] = query_grad
        g_ref[3 - 2 * me] = jnp.zeros_like(query_grad)
        write_terms(g_ref, u_ref, r_ref, [
            ((2, 1), (right_ref, 0), (right_ref, HS)),
            ((1, 2), (right_ref, N), (left_ref, N)),
            ((-1, 2), (right_ref, N + HS), (left_ref, N + HS)),
            ((2, -1), (left_ref, 0), (left_ref, HS)),
            ((2, 2), (across_ref, 0), (across_ref, HS)),
        ])

    shapes = [(2 * N, HS), (2 * N, HS), (N, HS), (4, HS, HS)]
    return call(body, [enc_lengths, dec_lengths, total, own_w, other_w], shapes, 60 * HS**3, BF16, 2)


def spread(grads, own_w, other_w):
    def body(g_ref, u_ref, r_ref, far, right, left, up, down, right_c, left_c, here):
        write_terms(g_ref, u_ref, r_ref, [
            ((2, 0), (far, 0), (far, HS)),
            ((1, 1), (right, 0), (right, HS)),
            ((-1, 1), (right, N), (right, N + HS)),
            ((1, -1), (left, 0), (left, HS)),
            ((-1, -1), (left, N), (left, N + HS)),
            ((0, 2), (right, 2 * N), (left, 2 * N)),
            ((1, 0), (up, 0), (up, HS)),
            ((-1, 0), (down, 0), (down, HS)),
            ((0, 1), (right_c, 0), (right_c, HS)),
            ((0, -1), (left_c, 0), (left_c, HS)),
            ((0, 0), (here, 0), (here, HS)),
        ])

    rows = [N, 2 * N + HS, 2 * N + HS, N, N, N, N, N]
    return call(body, [grads, own_w, other_w], [(r, HS) for r in rows], 88 * HS**3)


def add_rows(sources, rows, recipe):
    def body(*refs):
        ins, outs = refs[: len(sources)], refs[len(sources) :]
        for out, row, parts in recipe:
            value = ins[parts[0][0]][parts[0][1] : parts[0][1] + HS, :]
            if len(parts) > 1:
                value = value.astype(F32)
                for source, first in parts[1:]:
                    value += ins[source][first : first + HS, :].astype(F32)
            outs[out][row : row + HS, :] = value.astype(BF16)

    return call(body, list(sources), [(r, HS) for r in rows])


def finish(here, arrived, swapped):
    def body(here_ref, *rest):
        sec = lax.axis_index("section")
        value = here_ref[:HS, :].astype(F32)
        for ref in rest[: len(arrived)]:
            value += ref[:HS, :].astype(F32)
        rest[-1][slot_rows(sec), :] = value.astype(BF16)
        rest[-1][slot_rows(1 - sec), :] = rest[len(arrived)][...]

    return call(body, [here, *arrived, swapped], [(N, HS)])[0]


def local(states, proj_weights, out_cotangent, enc_lengths, dec_lengths):
    own = states[0]
    partner = lax.ppermute(own, "section", SWAP)
    c0 = assemble(own, out_cotangent, partner)

    up1, down1 = shift_y(c0, 1), shift_y(c0, -1)
    right0, left0, across0 = shift_x(c0, 1), shift_x(c0, -1), shift_x(c0, 2)
    c0, up1, down1, right0, left0, across0, own_w = lax.optimization_barrier(
        (c0, up1, down1, right0, left0, across0, proj_weights[0])
    )
    other_w = lax.ppermute(own_w, "section", SWAP)

    pair = jnp.concatenate([up1, down1], axis=0)
    right1, left1 = shift_x(pair, 1), shift_x(pair, -1)
    last = shift_y(c0, 2)
    total = project(
        [c0, pair, right0, left0, across0],
        [
            ((0, 0), [(0, 0, ROWS)]), ((-1, 0), [(1, 0, ROWS)]), ((1, 0), [(1, ROWS, ROWS)]),
            ((0, -1), [(2, 0, ROWS)]), ((0, 1), [(3, 0, ROWS)]), ((0, 2), [(4, 0, ROWS)]),
        ],
        own_w, other_w, None,
    )
    right1, left1, last, total = lax.optimization_barrier((right1, left1, last, total))

    right2 = shift_x(jnp.concatenate([right1[:HALF], right1[ROWS : ROWS + HALF], last], axis=0), 1)
    left2 = shift_x(jnp.concatenate([left1[HALF:ROWS], left1[ROWS + HALF :], last], axis=0), -1)
    across2 = shift_x(last, 2)
    total = project(
        [right1, left1, last],
        [
            ((-1, -1), [(0, 0, ROWS)]), ((1, -1), [(0, ROWS, ROWS)]),
            ((-1, 1), [(1, 0, ROWS)]), ((1, 1), [(1, ROWS, ROWS)]), ((2, 0), [(2, 0, ROWS)]),
        ],
        own_w, other_w, total,
    )
    right2, left2, across2, total = lax.optimization_barrier((right2, left2, across2, total))
    total = project(
        [right2, left2, across2],
        [
            ((-1, 2), [(0, 0, HALF), (1, 0, HALF)]), ((1, 2), [(0, HALF, HALF), (1, HALF, HALF)]),
            ((2, -1), [(0, ROWS, ROWS)]), ((2, 1), [(1, ROWS, ROWS)]), ((2, 2), [(2, 0, ROWS)]),
        ],
        own_w, other_w, total,
    )

    right_a, left_a, across_a, grads = attend(enc_lengths, dec_lengths, total, own_w, other_w)
    right_a, left_a, across_a = shift_x(right_a, 1), shift_x(left_a, -1), shift_x(across_a, 2)
    far, right_b, left_b, up_c, down_c, right_c, left_c, here = spread(grads, own_w, other_w)
    far, right_b, left_b = add_rows(
        [far, right_b, left_b, right_a, left_a, across_a], [N, 2 * N + HS, 2 * N + HS],
        [
            (0, 0, [(0, 0), (3, 0), (4, 0), (5, 0)]), (0, HS, [(0, HS), (3, HS), (4, HS), (5, HS)]),
            (1, 0, [(1, 0), (3, N)]), (1, HS, [(1, HS)]),
            (1, N, [(1, N), (3, N + HS)]), (1, N + HS, [(1, N + HS)]), (1, 2 * N, [(1, 2 * N)]),
            (2, 0, [(2, 0)]), (2, HS, [(2, HS), (4, N)]),
            (2, N, [(2, N)]), (2, N + HS, [(2, N + HS), (4, N + HS)]), (2, 2 * N, [(2, 2 * N)]),
        ],
    )
    far = shift_y(far, 2)
    right_b, left_b = shift_x(right_b, 1), shift_x(left_b, -1)
    up_c, down_c, right_c, left_c = add_rows(
        [up_c, down_c, right_c, left_c, right_b, left_b], [N] * 4,
        [
            (0, 0, [(0, 0), (4, 0), (5, 0)]), (0, HS, [(0, HS), (4, HS), (5, HS)]),
            (1, 0, [(1, 0), (4, N), (5, N)]), (1, HS, [(1, HS), (4, N + HS), (5, N + HS)]),
            (2, 0, [(2, 0), (4, 2 * N)]), (2, HS, [(2, HS)]),
            (3, 0, [(3, 0)]), (3, HS, [(3, HS), (5, 2 * N)]),
        ],
    )
    up_c, down_c, right_c, left_c = shift_y(up_c, 1), shift_y(down_c, -1), shift_x(right_c, 1), shift_x(left_c, -1)
    arrived = [far, up_c, down_c, right_c, left_c]
    sent = add_rows([here, *arrived], [HS], [(0, 0, [(i, HS) for i in range(6)])])[0]
    swapped = lax.ppermute(sent, "section", SWAP)
    return finish(here, arrived, swapped)[None]


def solution(mesh):
    placed = (
        P("section", "dp", "mp"),
        P("section", None, None, "mp"),
        P("dp", "mp"),
        P("dp"),
        P("dp"),
    )
    return jax.shard_map(
        local, mesh=mesh, in_specs=placed, out_specs=P("section", "dp", "mp"), check_vma=False
    )
```

```python
import jax
import jax.numpy as jnp
from jax import lax
from jax.experimental import pallas as pl
from jax.experimental.pallas import tpu as pltpu
from jax.sharding import PartitionSpec as P

HS = 256
SIDE = 4
ROWS = 3 * HS
HALF = ROWS // 2
N = 2 * HS
F32 = jnp.float32
BF16 = jnp.bfloat16
SWAP = [(0, 1), (1, 0)]
NT = (((1,), (1,)), ((), ()))
TN = (((0,), (0,)), ((), ()))
VMEM = pl.BlockSpec(memory_space=pltpu.VMEM)
SMEM = pl.BlockSpec(memory_space=pltpu.SMEM)
VMEM_LIMIT = 20 * 2**20


def shift_x(block, step):
    route = [(y * SIDE + x, y * SIDE + (x + step) % SIDE) for y in range(SIDE) for x in range(SIDE)]
    return lax.ppermute(block, "mp", route)


def shift_y(block, step):
    route = [(y * SIDE + x, (y + step) % SIDE * SIDE + x) for y in range(SIDE) for x in range(SIDE)]
    return lax.ppermute(block, "mp", route)


def join(*parts):
    return jnp.concatenate(parts, axis=0)


def call(body, inputs, shapes, flops=0, out_dtype=BF16, scalars=0):
    out = [jax.ShapeDtypeStruct(s, out_dtype) for s in shapes]
    moved = sum(a.size * a.dtype.itemsize for a in inputs)
    return pl.pallas_call(
        body,
        out_shape=out,
        in_specs=[SMEM] * scalars + [VMEM] * (len(inputs) - scalars),
        out_specs=[VMEM] * len(out),
        compiler_params=pltpu.CompilerParams(vmem_limit_bytes=VMEM_LIMIT),
        cost_estimate=pl.CostEstimate(flops=flops, bytes_accessed=moved, transcendentals=0),
    )(*inputs)


def feature_rows(offset):
    me = lax.axis_index("mp")
    y = lax.rem(lax.div(me, SIDE) + offset[0] + SIDE, SIDE)
    x = lax.rem(lax.rem(me, SIDE) + offset[1] + SIDE, SIDE)
    return pl.ds(pl.multiple_of((y * SIDE + x) * HS, HS), HS)


def slot_rows(index):
    return pl.ds(pl.multiple_of(index * HS, HS), HS)


def assemble(own, cotangent, partner):
    def body(own_ref, cot_ref, partner_ref, out_ref, sems):
        sec = lax.axis_index("section")
        here = slot_rows(sec)
        copies = [
            pltpu.make_async_copy(own_ref.at[here, :], out_ref.at[pl.ds(0, HS), :], sems.at[0]),
            pltpu.make_async_copy(cot_ref.at[here, :], out_ref.at[slot_rows(2 - sec), :], sems.at[1]),
        ]
        for copy in copies:
            copy.start()
        out_ref[slot_rows(1 + sec), :] = partner_ref[here, :]
        for copy in copies:
            copy.wait()

    return pl.pallas_call(
        body,
        out_shape=jax.ShapeDtypeStruct((ROWS, HS), BF16),
        in_specs=[pl.BlockSpec(memory_space=pltpu.HBM)] * 2 + [VMEM],
        out_specs=VMEM,
        scratch_shapes=[pltpu.SemaphoreType.DMA((2,))],
        compiler_params=pltpu.CompilerParams(vmem_limit_bytes=VMEM_LIMIT),
    )(own, cotangent, partner)


def rows_of(refs, block, low, high):
    parts, at = [], 0
    for which, first, count in block:
        a, b = max(low, at), min(high, at + count)
        if a < b:
            parts.append(refs[which][first + a - at : first + b - at, :])
        at += count
    return parts[0] if len(parts) == 1 else jnp.concatenate(parts, axis=0)


def project(pieces, blocks, own_w, other_w, total):
    def body(u_ref, r_ref, *rest):
        refs, out_ref = rest[: len(pieces)], rest[-1]
        core0 = lax.axis_index("section") == 0
        feats = [feature_rows(offset) for offset, _ in blocks]
        parts = [
            jnp.concatenate([rows_of(refs, block, k * HS, (k + 1) * HS) for _, block in blocks], axis=1)
            for k in range(3)
        ]
        lhs = (parts[0], jnp.where(core0, parts[0], parts[1]), jnp.where(core0, parts[1], parts[2]), parts[2])
        for j in range(4):
            w_ref = (u_ref, r_ref)[j // 2]
            weight = jnp.concatenate([w_ref[j % 2, f, :] for f in feats], axis=0)
            term = jnp.dot(lhs[j], weight, preferred_element_type=F32)
            out_ref[j] = term if total is None else rest[-2][j] + term

    inputs = [own_w, other_w, *pieces] + ([] if total is None else [total])
    return call(body, inputs, [(4, HS, HS)], len(blocks) * 8 * HS**3, F32)[0]


def write_terms(g_ref, u_ref, r_ref, wanted):
    for offset, *slots in wanted:
        feats = feature_rows(offset)
        for slot, (out_ref, row) in enumerate(slots):
            w_ref = (u_ref, r_ref)[slot]
            term = lax.dot_general(g_ref[2 * slot], w_ref[0, feats, :], NT, preferred_element_type=F32)
            term += lax.dot_general(g_ref[2 * slot + 1], w_ref[1, feats, :], NT, preferred_element_type=F32)
            out_ref[row : row + HS, :] = term.astype(BF16)


def attend(enc_lengths, dec_lengths, total, own_w, other_w):
    scale = 1.0 / HS**0.5

    def body(enc_ref, dec_ref, t_ref, u_ref, r_ref, right_ref, left_ref, across_ref, g_ref):
        me = lax.axis_index("section")
        keys = t_ref[2 * me].astype(BF16)
        values = t_ref[2 * me + 1].astype(BF16)
        queries = t_ref[2 - 2 * me].astype(BF16)
        out_grad = t_ref[3 - 2 * me]
        live_q = lax.broadcasted_iota(jnp.int32, (HS, HS), 0) < dec_ref[me]
        live_k = lax.broadcasted_iota(jnp.int32, (HS, HS), 1) < enc_ref[me]
        masked = jnp.where(live_q, out_grad, 0.0).astype(BF16)
        scores = lax.dot_general(queries, keys, NT, preferred_element_type=F32) * scale
        scores = jnp.where(live_k, scores, -1e30)
        top = jnp.max(scores, axis=-1, keepdims=True)
        expd = jnp.exp(scores - top)
        probs = expd / jnp.sum(expd, axis=-1, keepdims=True)
        value_grad = lax.dot_general(probs.astype(BF16), masked, TN, preferred_element_type=F32).astype(BF16)
        prob_grad = lax.dot_general(masked, values, NT, preferred_element_type=F32)
        delta = jnp.sum(probs * prob_grad, axis=-1, keepdims=True)
        sg = (probs * (prob_grad - delta)).astype(BF16)
        query_grad = (jnp.dot(sg, keys, preferred_element_type=F32) * scale).astype(BF16)
        key_grad = (lax.dot_general(sg, queries, TN, preferred_element_type=F32) * scale).astype(BF16)
        g_ref[2 * me] = key_grad
        g_ref[2 * me + 1] = value_grad
        g_ref[2 - 2 * me] = query_grad
        g_ref[3 - 2 * me] = jnp.zeros_like(query_grad)
        write_terms(g_ref, u_ref, r_ref, [
            ((2, 1), (right_ref, 0), (right_ref, HS)),
            ((1, 2), (right_ref, N), (left_ref, N)),
            ((-1, 2), (right_ref, N + HS), (left_ref, N + HS)),
            ((2, -1), (left_ref, 0), (left_ref, HS)),
            ((2, 2), (across_ref, 0), (across_ref, HS)),
        ])

    shapes = [(2 * N, HS), (2 * N, HS), (N, HS), (4, HS, HS)]
    return call(body, [enc_lengths, dec_lengths, total, own_w, other_w], shapes, 60 * HS**3, BF16, 2)


def spread(grads, own_w, other_w):
    def body(g_ref, u_ref, r_ref, far, right, left, up, down, right_c, left_c, here):
        write_terms(g_ref, u_ref, r_ref, [
            ((2, 0), (far, 0), (far, HS)),
            ((1, 1), (right, 0), (right, HS)),
            ((-1, 1), (right, N), (right, N + HS)),
            ((1, -1), (left, 0), (left, HS)),
            ((-1, -1), (left, N), (left, N + HS)),
            ((0, 2), (right, 2 * N), (left, 2 * N)),
            ((1, 0), (up, 0), (up, HS)),
            ((-1, 0), (down, 0), (down, HS)),
            ((0, 1), (right_c, 0), (right_c, HS)),
            ((0, -1), (left_c, 0), (left_c, HS)),
            ((0, 0), (here, 0), (here, HS)),
        ])

    rows = [N, 2 * N + HS, 2 * N + HS, N, N, N, N, N]
    return call(body, [grads, own_w, other_w], [(r, HS) for r in rows], 88 * HS**3)


def add_rows(sources, rows, recipe):
    def body(*refs):
        ins, outs = refs[: len(sources)], refs[len(sources) :]
        for out, row, parts in recipe:
            value = ins[parts[0][0]][parts[0][1] : parts[0][1] + HS, :]
            if len(parts) > 1:
                value = value.astype(F32)
                for source, first in parts[1:]:
                    value += ins[source][first : first + HS, :].astype(F32)
            outs[out][row : row + HS, :] = value.astype(BF16)

    return call(body, list(sources), [(r, HS) for r in rows])


def finish(here, arrived, swapped):
    def body(here_ref, *rest):
        sec = lax.axis_index("section")
        value = here_ref[:HS, :].astype(F32)
        for ref in rest[: len(arrived)]:
            value += ref[:HS, :].astype(F32)
        rest[-1][slot_rows(sec), :] = value.astype(BF16)
        rest[-1][slot_rows(1 - sec), :] = rest[len(arrived)][...]

    return call(body, [here, *arrived, swapped], [(N, HS)])[0]


def local(states, proj_weights, out_cotangent, enc_lengths, dec_lengths):
    own = states[0]
    partner = lax.ppermute(own, "section", SWAP)
    c0 = assemble(own, out_cotangent, partner)

    up1, down1 = shift_y(c0, 1), shift_y(c0, -1)
    right0, left0 = shift_x(c0, 1), shift_x(c0, -1)
    c0, up1, down1, right0, left0, own_w = lax.optimization_barrier(
        (c0, up1, down1, right0, left0, proj_weights[0])
    )
    other_w = lax.ppermute(own_w, "section", SWAP)

    right1 = shift_x(join(right0[:HALF], up1, down1[:HALF]), 1)
    left1 = shift_x(join(left0[HALF:], up1[HALF:], down1), -1)
    up2 = shift_y(join(up1[:HALF], left0[:HALF]), 1)
    down2 = shift_y(join(down1[HALF:], right0[HALF:]), -1)
    total = project(
        [c0, up1, down1, right0, left0],
        [
            ((0, 0), [(0, 0, ROWS)]), ((-1, 0), [(1, 0, ROWS)]), ((1, 0), [(2, 0, ROWS)]),
            ((0, -1), [(3, 0, ROWS)]), ((0, 1), [(4, 0, ROWS)]),
        ],
        own_w, other_w, None,
    )
    right1, left1, up2, down2, total = lax.optimization_barrier((right1, left1, up2, down2, total))

    last = join(up2[:HALF], down2[:HALF])
    right2 = shift_x(join(right1[HALF:ROWS], right1[ROWS + HALF :], last), 1)
    left2 = shift_x(join(left1[HALF:ROWS], left1[ROWS + HALF :], last), -1)
    across2 = shift_x(last, 2)
    total = project(
        [right1, left1, up2, down2],
        [
            ((-1, -1), [(0, HALF, ROWS)]), ((1, -1), [(0, HALF + ROWS, HALF), (3, HALF, HALF)]),
            ((-1, 1), [(2, HALF, HALF), (1, HALF, HALF)]), ((1, 1), [(1, ROWS, ROWS)]),
            ((0, 2), [(0, 0, HALF), (1, 0, HALF)]), ((2, 0), [(2, 0, HALF), (3, 0, HALF)]),
        ],
        own_w, other_w, total,
    )
    right2, left2, across2, total = lax.optimization_barrier((right2, left2, across2, total))
    total = project(
        [right2, left2, across2],
        [
            ((-1, 2), [(0, 0, HALF), (1, 0, HALF)]), ((1, 2), [(0, HALF, HALF), (1, HALF, HALF)]),
            ((2, -1), [(0, ROWS, ROWS)]), ((2, 1), [(1, ROWS, ROWS)]), ((2, 2), [(2, 0, ROWS)]),
        ],
        own_w, other_w, total,
    )

    right_a, left_a, across_a, grads = attend(enc_lengths, dec_lengths, total, own_w, other_w)
    right_a, left_a, across_a = shift_x(right_a, 1), shift_x(left_a, -1), shift_x(across_a, 2)
    far, right_b, left_b, up_c, down_c, right_c, left_c, here = spread(grads, own_w, other_w)
    far, right_b, left_b = add_rows(
        [far, right_b, left_b, right_a, left_a, across_a], [N, 2 * N + HS, 2 * N + HS],
        [
            (0, 0, [(0, 0), (3, 0), (4, 0), (5, 0)]), (0, HS, [(0, HS), (3, HS), (4, HS), (5, HS)]),
            (1, 0, [(1, 0), (3, N)]), (1, HS, [(1, HS)]),
            (1, N, [(1, N), (3, N + HS)]), (1, N + HS, [(1, N + HS)]), (1, 2 * N, [(1, 2 * N)]),
            (2, 0, [(2, 0)]), (2, HS, [(2, HS), (4, N)]),
            (2, N, [(2, N)]), (2, N + HS, [(2, N + HS), (4, N + HS)]), (2, 2 * N, [(2, 2 * N)]),
        ],
    )
    far = shift_y(far, 2)
    right_b, left_b = shift_x(right_b, 1), shift_x(left_b, -1)
    up_c, down_c, right_c, left_c = add_rows(
        [up_c, down_c, right_c, left_c, right_b, left_b], [N] * 4,
        [
            (0, 0, [(0, 0), (4, 0), (5, 0)]), (0, HS, [(0, HS), (4, HS), (5, HS)]),
            (1, 0, [(1, 0), (4, N), (5, N)]), (1, HS, [(1, HS), (4, N + HS), (5, N + HS)]),
            (2, 0, [(2, 0), (4, 2 * N)]), (2, HS, [(2, HS)]),
            (3, 0, [(3, 0)]), (3, HS, [(3, HS), (5, 2 * N)]),
        ],
    )
    up_c, down_c, right_c, left_c = shift_y(up_c, 1), shift_y(down_c, -1), shift_x(right_c, 1), shift_x(left_c, -1)
    arrived = [far, up_c, down_c, right_c, left_c]
    sent = add_rows([here, *arrived], [HS], [(0, 0, [(i, HS) for i in range(6)])])[0]
    swapped = lax.ppermute(sent, "section", SWAP)
    return finish(here, arrived, swapped)[None]


def solution(mesh):
    placed = (
        P("section", "dp", "mp"),
        P("section", None, None, "mp"),
        P("dp", "mp"),
        P("dp"),
        P("dp"),
    )
    return jax.shard_map(
        local, mesh=mesh, in_specs=placed, out_specs=P("section", "dp", "mp"), check_vma=False
    )
```

```python
import jax
import jax.numpy as jnp
from jax import lax
from jax.experimental import pallas as pl
from jax.experimental.pallas import tpu as pltpu
from jax.sharding import PartitionSpec as P

HS = 256
SIDE = 4
ROWS = 3 * HS
HALF = ROWS // 2
REST = ROWS // 4
MOST = ROWS - REST
N = 2 * HS
F32 = jnp.float32
BF16 = jnp.bfloat16
SWAP = [(0, 1), (1, 0)]
NT = (((1,), (1,)), ((), ()))
TN = (((0,), (0,)), ((), ()))
VMEM = pl.BlockSpec(memory_space=pltpu.VMEM)
SMEM = pl.BlockSpec(memory_space=pltpu.SMEM)
VMEM_LIMIT = 20 * 2**20


def shift_x(block, step):
    route = [(y * SIDE + x, y * SIDE + (x + step) % SIDE) for y in range(SIDE) for x in range(SIDE)]
    return lax.ppermute(block, "mp", route)


def shift_y(block, step):
    route = [(y * SIDE + x, (y + step) % SIDE * SIDE + x) for y in range(SIDE) for x in range(SIDE)]
    return lax.ppermute(block, "mp", route)


def join(*parts):
    return jnp.concatenate(parts, axis=0)


def call(body, inputs, shapes, flops=0, out_dtype=BF16, scalars=0):
    out = [jax.ShapeDtypeStruct(s, out_dtype) for s in shapes]
    moved = sum(a.size * a.dtype.itemsize for a in inputs)
    return pl.pallas_call(
        body,
        out_shape=out,
        in_specs=[SMEM] * scalars + [VMEM] * (len(inputs) - scalars),
        out_specs=[VMEM] * len(out),
        compiler_params=pltpu.CompilerParams(vmem_limit_bytes=VMEM_LIMIT),
        cost_estimate=pl.CostEstimate(flops=flops, bytes_accessed=moved, transcendentals=0),
    )(*inputs)


def feature_rows(offset):
    me = lax.axis_index("mp")
    y = lax.rem(lax.div(me, SIDE) + offset[0] + SIDE, SIDE)
    x = lax.rem(lax.rem(me, SIDE) + offset[1] + SIDE, SIDE)
    return pl.ds(pl.multiple_of((y * SIDE + x) * HS, HS), HS)


def slot_rows(index):
    return pl.ds(pl.multiple_of(index * HS, HS), HS)


def local_rows(own, cotangent):
    def body(own_ref, cot_ref, out_ref):
        here = slot_rows(lax.axis_index("section"))
        out_ref[:HS, :] = own_ref[here, :]
        out_ref[HS:, :] = cot_ref[here, :]

    return call(body, [own, cotangent], [(N, HS)])[0]


def assemble(local, partner):
    def body(local_ref, partner_ref, out_ref):
        sec = lax.axis_index("section")
        out_ref[:HS, :] = local_ref[:HS, :]
        out_ref[slot_rows(2 - sec), :] = local_ref[HS:, :]
        out_ref[slot_rows(1 + sec), :] = partner_ref[slot_rows(sec), :]

    return call(body, [local, partner], [(ROWS, HS)])[0]


def rows_of(refs, block, low, high):
    parts, at = [], 0
    for which, first, count in block:
        a, b = max(low, at), min(high, at + count)
        if a < b:
            parts.append(refs[which][first + a - at : first + b - at, :])
        at += count
    return parts[0] if len(parts) == 1 else jnp.concatenate(parts, axis=0)


def project(pieces, blocks, own_w, other_w, total):
    def body(u_ref, r_ref, *rest):
        refs, out_ref = rest[: len(pieces)], rest[-1]
        core0 = lax.axis_index("section") == 0
        feats = [feature_rows(offset) for offset, _ in blocks]
        parts = [
            jnp.concatenate([rows_of(refs, block, k * HS, (k + 1) * HS) for _, block in blocks], axis=1)
            for k in range(3)
        ]
        lhs = (parts[0], jnp.where(core0, parts[0], parts[1]), jnp.where(core0, parts[1], parts[2]), parts[2])
        for j in range(4):
            w_ref = (u_ref, r_ref)[j // 2]
            weight = jnp.concatenate([w_ref[j % 2, f, :] for f in feats], axis=0)
            term = jnp.dot(lhs[j], weight, preferred_element_type=F32)
            out_ref[j] = term if total is None else rest[-2][j] + term

    inputs = [own_w, other_w, *pieces] + ([] if total is None else [total])
    return call(body, inputs, [(4, HS, HS)], len(blocks) * 8 * HS**3, F32)[0]


def write_terms(g_ref, u_ref, r_ref, wanted):
    for offset, *slots in wanted:
        feats = feature_rows(offset)
        for slot, (out_ref, row) in enumerate(slots):
            w_ref = (u_ref, r_ref)[slot]
            term = lax.dot_general(g_ref[2 * slot], w_ref[0, feats, :], NT, preferred_element_type=F32)
            term += lax.dot_general(g_ref[2 * slot + 1], w_ref[1, feats, :], NT, preferred_element_type=F32)
            out_ref[row : row + HS, :] = term.astype(BF16)


def attend(enc_lengths, dec_lengths, total, own_w, other_w):
    scale = 1.0 / HS**0.5

    def body(enc_ref, dec_ref, t_ref, u_ref, r_ref, right_ref, left_ref, across_ref, g_ref):
        me = lax.axis_index("section")
        keys = t_ref[2 * me].astype(BF16)
        values = t_ref[2 * me + 1].astype(BF16)
        queries = t_ref[2 - 2 * me].astype(BF16)
        out_grad = t_ref[3 - 2 * me]
        live_q = lax.broadcasted_iota(jnp.int32, (HS, HS), 0) < dec_ref[me]
        live_k = lax.broadcasted_iota(jnp.int32, (HS, HS), 1) < enc_ref[me]
        masked = jnp.where(live_q, out_grad, 0.0).astype(BF16)
        scores = lax.dot_general(queries, keys, NT, preferred_element_type=F32) * scale
        scores = jnp.where(live_k, scores, -1e30)
        top = jnp.max(scores, axis=-1, keepdims=True)
        expd = jnp.exp(scores - top)
        probs = expd / jnp.sum(expd, axis=-1, keepdims=True)
        value_grad = lax.dot_general(probs.astype(BF16), masked, TN, preferred_element_type=F32).astype(BF16)
        prob_grad = lax.dot_general(masked, values, NT, preferred_element_type=F32)
        delta = jnp.sum(probs * prob_grad, axis=-1, keepdims=True)
        sg = (probs * (prob_grad - delta)).astype(BF16)
        query_grad = (jnp.dot(sg, keys, preferred_element_type=F32) * scale).astype(BF16)
        key_grad = (lax.dot_general(sg, queries, TN, preferred_element_type=F32) * scale).astype(BF16)
        g_ref[2 * me] = key_grad
        g_ref[2 * me + 1] = value_grad
        g_ref[2 - 2 * me] = query_grad
        g_ref[3 - 2 * me] = jnp.zeros_like(query_grad)
        write_terms(g_ref, u_ref, r_ref, [
            ((2, 1), (right_ref, 0), (right_ref, HS)),
            ((1, 2), (right_ref, N), (left_ref, N)),
            ((-1, 2), (right_ref, N + HS), (left_ref, N + HS)),
            ((2, -1), (left_ref, 0), (left_ref, HS)),
            ((2, 2), (across_ref, 0), (across_ref, HS)),
        ])

    shapes = [(2 * N, HS), (2 * N, HS), (N, HS), (4, HS, HS)]
    return call(body, [enc_lengths, dec_lengths, total, own_w, other_w], shapes, 60 * HS**3, BF16, 2)


def spread(grads, own_w, other_w):
    def body(g_ref, u_ref, r_ref, far, right, left, up, down, right_c, left_c, here):
        write_terms(g_ref, u_ref, r_ref, [
            ((2, 0), (far, 0), (far, HS)),
            ((1, 1), (right, 0), (right, HS)),
            ((-1, 1), (right, N), (right, N + HS)),
            ((1, -1), (left, 0), (left, HS)),
            ((-1, -1), (left, N), (left, N + HS)),
            ((0, 2), (right, 2 * N), (left, 2 * N)),
            ((1, 0), (up, 0), (up, HS)),
            ((-1, 0), (down, 0), (down, HS)),
            ((0, 1), (right_c, 0), (right_c, HS)),
            ((0, -1), (left_c, 0), (left_c, HS)),
            ((0, 0), (here, 0), (here, HS)),
        ])

    rows = [N, 2 * N + HS, 2 * N + HS, N, N, N, N, N]
    return call(body, [grads, own_w, other_w], [(r, HS) for r in rows], 88 * HS**3)


def add_rows(sources, rows, recipe):
    def body(*refs):
        ins, outs = refs[: len(sources)], refs[len(sources) :]
        for out, row, parts in recipe:
            value = ins[parts[0][0]][parts[0][1] : parts[0][1] + HS, :]
            if len(parts) > 1:
                value = value.astype(F32)
                for source, first in parts[1:]:
                    value += ins[source][first : first + HS, :].astype(F32)
            outs[out][row : row + HS, :] = value.astype(BF16)

    return call(body, list(sources), [(r, HS) for r in rows])


def finish(here, arrived, swapped):
    def body(here_ref, *rest):
        sec = lax.axis_index("section")
        value = here_ref[:HS, :].astype(F32)
        for ref in rest[: len(arrived)]:
            value += ref[:HS, :].astype(F32)
        rest[-1][slot_rows(sec), :] = value.astype(BF16)
        rest[-1][slot_rows(1 - sec), :] = rest[len(arrived)][...]

    return call(body, [here, *arrived, swapped], [(N, HS)])[0]


def local(states, proj_weights, out_cotangent, enc_lengths, dec_lengths):
    own = states[0]
    partner = lax.ppermute(own, "section", SWAP)
    c0 = assemble(local_rows(own, out_cotangent), partner)

    up1, down1 = shift_y(c0, 1), shift_y(c0, -1)
    right0, left0 = shift_x(c0, 1), shift_x(c0, -1)
    c0, up1, down1, right0, left0, own_w = lax.optimization_barrier(
        (c0, up1, down1, right0, left0, proj_weights[0])
    )
    other_w = lax.ppermute(own_w, "section", SWAP)

    right1 = shift_x(join(right0[:HALF], up1, down1[:HALF]), 1)
    left1 = shift_x(join(left0[HALF:], up1[HALF:], down1), -1)
    up2 = shift_y(join(up1[:HALF], left0[:HALF]), 1)
    down2 = shift_y(join(down1[HALF:], right0[HALF:]), -1)
    total = project(
        [c0, up1, down1, right0, left0],
        [
            ((0, 0), [(0, 0, ROWS)]), ((-1, 0), [(1, 0, ROWS)]), ((1, 0), [(2, 0, ROWS)]),
            ((0, -1), [(3, 0, ROWS)]), ((0, 1), [(4, 0, ROWS)]),
        ],
        own_w, other_w, None,
    )
    right1, left1, up2, down2, total = lax.optimization_barrier((right1, left1, up2, down2, total))

    last = join(up2[:HALF], down2[:HALF])
    right2 = shift_x(join(right1[HALF : HALF + MOST], right1[ROWS + HALF :], down2[HALF : HALF + REST]), 1)
    left2 = shift_x(join(left1[HALF + REST : ROWS], left1[ROWS + MOST :], last), -1)
    up3, down3 = shift_y(right1[HALF:ROWS], 1), shift_y(down2[HALF:], -1)
    across2 = shift_x(last, 2)
    total = project(
        [right1, left1, up2, down2],
        [
            ((-1, -1), [(0, HALF, ROWS)]), ((1, -1), [(0, HALF + ROWS, HALF), (3, HALF, HALF)]),
            ((-1, 1), [(2, HALF, HALF), (1, HALF, HALF)]), ((1, 1), [(1, ROWS, ROWS)]),
            ((0, 2), [(0, 0, HALF), (1, 0, HALF)]), ((2, 0), [(2, 0, HALF), (3, 0, HALF)]),
        ],
        own_w, other_w, total,
    )
    right2, left2, across2, up3, down3, total = lax.optimization_barrier(
        (right2, left2, across2, up3, down3, total)
    )
    total = project(
        [right2, left2, across2, up3, down3],
        [
            ((-1, 2), [(0, 0, MOST), (1, 0, REST)]), ((1, 2), [(0, MOST, MOST), (1, REST, REST)]),
            ((2, -1), [(3, 0, HALF), (4, 0, HALF)]), ((2, 1), [(1, 2 * REST, ROWS)]), ((2, 2), [(2, 0, ROWS)]),
        ],
        own_w, other_w, total,
    )

    right_a, left_a, across_a, grads = attend(enc_lengths, dec_lengths, total, own_w, other_w)
    right_a, left_a, across_a = shift_x(right_a, 1), shift_x(left_a, -1), shift_x(across_a, 2)
    far, right_b, left_b, up_c, down_c, right_c, left_c, here = spread(grads, own_w, other_w)
    far, right_b, left_b = add_rows(
        [far, right_b, left_b, right_a, left_a, across_a], [N, 2 * N + HS, 2 * N + HS],
        [
            (0, 0, [(0, 0), (3, 0), (4, 0), (5, 0)]), (0, HS, [(0, HS), (3, HS), (4, HS), (5, HS)]),
            (1, 0, [(1, 0), (3, N)]), (1, HS, [(1, HS)]),
            (1, N, [(1, N), (3, N + HS)]), (1, N + HS, [(1, N + HS)]), (1, 2 * N, [(1, 2 * N)]),
            (2, 0, [(2, 0)]), (2, HS, [(2, HS), (4, N)]),
            (2, N, [(2, N)]), (2, N + HS, [(2, N + HS), (4, N + HS)]), (2, 2 * N, [(2, 2 * N)]),
        ],
    )
    far = shift_y(far, 2)
    right_b, left_b = shift_x(right_b, 1), shift_x(left_b, -1)
    up_c, down_c, right_c, left_c = add_rows(
        [up_c, down_c, right_c, left_c, right_b, left_b], [N] * 4,
        [
            (0, 0, [(0, 0), (4, 0), (5, 0)]), (0, HS, [(0, HS), (4, HS), (5, HS)]),
            (1, 0, [(1, 0), (4, N), (5, N)]), (1, HS, [(1, HS), (4, N + HS), (5, N + HS)]),
            (2, 0, [(2, 0), (4, 2 * N)]), (2, HS, [(2, HS)]),
            (3, 0, [(3, 0)]), (3, HS, [(3, HS), (5, 2 * N)]),
        ],
    )
    up_c, down_c, right_c, left_c = shift_y(up_c, 1), shift_y(down_c, -1), shift_x(right_c, 1), shift_x(left_c, -1)
    arrived = [far, up_c, down_c, right_c, left_c]
    sent = add_rows([here, *arrived], [HS], [(0, 0, [(i, HS) for i in range(6)])])[0]
    swapped = lax.ppermute(sent, "section", SWAP)
    return finish(here, arrived, swapped)[None]


def solution(mesh):
    placed = (
        P("section", "dp", "mp"),
        P("section", None, None, "mp"),
        P("dp", "mp"),
        P("dp"),
        P("dp"),
    )
    return jax.shard_map(
        local, mesh=mesh, in_specs=placed, out_specs=P("section", "dp", "mp"), check_vma=False
    )
```

```python
import jax
import jax.numpy as jnp
from jax import lax
from jax.experimental import pallas as pl
from jax.experimental.pallas import tpu as pltpu
from jax.sharding import PartitionSpec as P

HS = 256
SIDE = 4
ROWS = 3 * HS
HALF = ROWS // 2
D = 192
E = 96
MOST = 528
REST = ROWS - MOST
N = 2 * HS
F32 = jnp.float32
BF16 = jnp.bfloat16
SWAP = [(0, 1), (1, 0)]
NT = (((1,), (1,)), ((), ()))
TN = (((0,), (0,)), ((), ()))
VMEM = pl.BlockSpec(memory_space=pltpu.VMEM)
SMEM = pl.BlockSpec(memory_space=pltpu.SMEM)
VMEM_LIMIT = 20 * 2**20


def shift_x(block, step):
    route = [(y * SIDE + x, y * SIDE + (x + step) % SIDE) for y in range(SIDE) for x in range(SIDE)]
    return lax.ppermute(block, "mp", route)


def shift_y(block, step):
    route = [(y * SIDE + x, (y + step) % SIDE * SIDE + x) for y in range(SIDE) for x in range(SIDE)]
    return lax.ppermute(block, "mp", route)


def join(*parts):
    return jnp.concatenate(parts, axis=0)


def call(body, inputs, shapes, flops=0, out_dtype=BF16, scalars=0):
    out = [jax.ShapeDtypeStruct(s, out_dtype) for s in shapes]
    moved = sum(a.size * a.dtype.itemsize for a in inputs)
    return pl.pallas_call(
        body,
        out_shape=out,
        in_specs=[SMEM] * scalars + [VMEM] * (len(inputs) - scalars),
        out_specs=[VMEM] * len(out),
        compiler_params=pltpu.CompilerParams(vmem_limit_bytes=VMEM_LIMIT),
        cost_estimate=pl.CostEstimate(flops=flops, bytes_accessed=moved, transcendentals=0),
    )(*inputs)


def feature_rows(offset):
    me = lax.axis_index("mp")
    y = lax.rem(lax.div(me, SIDE) + offset[0] + SIDE, SIDE)
    x = lax.rem(lax.rem(me, SIDE) + offset[1] + SIDE, SIDE)
    return pl.ds(pl.multiple_of((y * SIDE + x) * HS, HS), HS)


def slot_rows(index):
    return pl.ds(pl.multiple_of(index * HS, HS), HS)


def local_rows(own, cotangent):
    def body(own_ref, cot_ref, out_ref):
        here = slot_rows(lax.axis_index("section"))
        out_ref[:HS, :] = own_ref[here, :]
        out_ref[HS:, :] = cot_ref[here, :]

    return call(body, [own, cotangent], [(N, HS)])[0]


def assemble(local, partner):
    def body(local_ref, partner_ref, out_ref):
        sec = lax.axis_index("section")
        out_ref[:HS, :] = local_ref[:HS, :]
        out_ref[slot_rows(2 - sec), :] = local_ref[HS:, :]
        out_ref[slot_rows(1 + sec), :] = partner_ref[slot_rows(sec), :]

    return call(body, [local, partner], [(ROWS, HS)])[0]


def rows_of(refs, block, low, high):
    parts, at = [], 0
    for which, first, count in block:
        a, b = max(low, at), min(high, at + count)
        if a < b:
            parts.append(refs[which][first + a - at : first + b - at, :])
        at += count
    return parts[0] if len(parts) == 1 else jnp.concatenate(parts, axis=0)


def project(pieces, blocks, own_w, other_w, total):
    def body(u_ref, r_ref, *rest):
        refs, out_ref = rest[: len(pieces)], rest[-1]
        core0 = lax.axis_index("section") == 0
        feats = [feature_rows(offset) for offset, _ in blocks]
        parts = [
            jnp.concatenate([rows_of(refs, block, k * HS, (k + 1) * HS) for _, block in blocks], axis=1)
            for k in range(3)
        ]
        lhs = (parts[0], jnp.where(core0, parts[0], parts[1]), jnp.where(core0, parts[1], parts[2]), parts[2])
        for j in range(4):
            w_ref = (u_ref, r_ref)[j // 2]
            weight = jnp.concatenate([w_ref[j % 2, f, :] for f in feats], axis=0)
            term = jnp.dot(lhs[j], weight, preferred_element_type=F32)
            out_ref[j] = term if total is None else rest[-2][j] + term

    inputs = [own_w, other_w, *pieces] + ([] if total is None else [total])
    return call(body, inputs, [(4, HS, HS)], len(blocks) * 8 * HS**3, F32)[0]


def write_terms(g_ref, u_ref, r_ref, wanted):
    for offset, *slots in wanted:
        feats = feature_rows(offset)
        for slot, (out_ref, row) in enumerate(slots):
            w_ref = (u_ref, r_ref)[slot]
            term = lax.dot_general(g_ref[2 * slot], w_ref[0, feats, :], NT, preferred_element_type=F32)
            term += lax.dot_general(g_ref[2 * slot + 1], w_ref[1, feats, :], NT, preferred_element_type=F32)
            out_ref[row : row + HS, :] = term.astype(BF16)


def attend(enc_lengths, dec_lengths, total, own_w, other_w):
    scale = 1.0 / HS**0.5

    def body(enc_ref, dec_ref, t_ref, u_ref, r_ref, right_ref, left_ref, across_ref, g_ref):
        me = lax.axis_index("section")
        keys = t_ref[2 * me].astype(BF16)
        values = t_ref[2 * me + 1].astype(BF16)
        queries = t_ref[2 - 2 * me].astype(BF16)
        out_grad = t_ref[3 - 2 * me]
        live_q = lax.broadcasted_iota(jnp.int32, (HS, HS), 0) < dec_ref[me]
        live_k = lax.broadcasted_iota(jnp.int32, (HS, HS), 1) < enc_ref[me]
        masked = jnp.where(live_q, out_grad, 0.0).astype(BF16)
        scores = lax.dot_general(queries, keys, NT, preferred_element_type=F32) * scale
        scores = jnp.where(live_k, scores, -1e30)
        top = jnp.max(scores, axis=-1, keepdims=True)
        expd = jnp.exp(scores - top)
        probs = expd / jnp.sum(expd, axis=-1, keepdims=True)
        value_grad = lax.dot_general(probs.astype(BF16), masked, TN, preferred_element_type=F32).astype(BF16)
        prob_grad = lax.dot_general(masked, values, NT, preferred_element_type=F32)
        delta = jnp.sum(probs * prob_grad, axis=-1, keepdims=True)
        sg = (probs * (prob_grad - delta)).astype(BF16)
        query_grad = (jnp.dot(sg, keys, preferred_element_type=F32) * scale).astype(BF16)
        key_grad = (lax.dot_general(sg, queries, TN, preferred_element_type=F32) * scale).astype(BF16)
        g_ref[2 * me] = key_grad
        g_ref[2 * me + 1] = value_grad
        g_ref[2 - 2 * me] = query_grad
        g_ref[3 - 2 * me] = jnp.zeros_like(query_grad)
        write_terms(g_ref, u_ref, r_ref, [
            ((2, 1), (right_ref, 0), (right_ref, HS)),
            ((1, 2), (right_ref, N), (left_ref, N)),
            ((-1, 2), (right_ref, N + HS), (left_ref, N + HS)),
            ((2, -1), (left_ref, 0), (left_ref, HS)),
            ((2, 2), (across_ref, 0), (across_ref, HS)),
        ])

    shapes = [(2 * N, HS), (2 * N, HS), (N, HS), (4, HS, HS)]
    return call(body, [enc_lengths, dec_lengths, total, own_w, other_w], shapes, 60 * HS**3, BF16, 2)


def spread(grads, own_w, other_w):
    def body(g_ref, u_ref, r_ref, far, right, left, up, down, right_c, left_c, here):
        write_terms(g_ref, u_ref, r_ref, [
            ((2, 0), (far, 0), (far, HS)),
            ((1, 1), (right, 0), (right, HS)),
            ((-1, 1), (right, N), (right, N + HS)),
            ((1, -1), (left, 0), (left, HS)),
            ((-1, -1), (left, N), (left, N + HS)),
            ((0, 2), (right, 2 * N), (left, 2 * N)),
            ((1, 0), (up, 0), (up, HS)),
            ((-1, 0), (down, 0), (down, HS)),
            ((0, 1), (right_c, 0), (right_c, HS)),
            ((0, -1), (left_c, 0), (left_c, HS)),
            ((0, 0), (here, 0), (here, HS)),
        ])

    rows = [N, 2 * N + HS, 2 * N + HS, N, N, N, N, N]
    return call(body, [grads, own_w, other_w], [(r, HS) for r in rows], 88 * HS**3)


def add_rows(sources, rows, recipe):
    def body(*refs):
        ins, outs = refs[: len(sources)], refs[len(sources) :]
        for out, row, parts in recipe:
            value = ins[parts[0][0]][parts[0][1] : parts[0][1] + HS, :]
            if len(parts) > 1:
                value = value.astype(F32)
                for source, first in parts[1:]:
                    value += ins[source][first : first + HS, :].astype(F32)
            outs[out][row : row + HS, :] = value.astype(BF16)

    return call(body, list(sources), [(r, HS) for r in rows])


def finish(here, arrived, swapped):
    def body(here_ref, *rest):
        sec = lax.axis_index("section")
        value = here_ref[:HS, :].astype(F32)
        for ref in rest[: len(arrived)]:
            value += ref[:HS, :].astype(F32)
        rest[-1][slot_rows(sec), :] = value.astype(BF16)
        rest[-1][slot_rows(1 - sec), :] = rest[len(arrived)][...]

    return call(body, [here, *arrived, swapped], [(N, HS)])[0]


def local(states, proj_weights, out_cotangent, enc_lengths, dec_lengths):
    own = states[0]
    partner = lax.ppermute(own, "section", SWAP)
    c0 = assemble(local_rows(own, out_cotangent), partner)

    up1, down1 = shift_y(c0, 1), shift_y(c0, -1)
    right0, left0 = shift_x(c0, 1), shift_x(c0, -1)
    c0, up1, down1, right0, left0, own_w = lax.optimization_barrier(
        (c0, up1, down1, right0, left0, proj_weights[0])
    )
    other_w = lax.ppermute(own_w, "section", SWAP)

    right1 = shift_x(join(right0[:HALF], up1, down1[: ROWS - D]), 1)
    left1 = shift_x(join(left0[HALF:], up1[D:], down1), -1)
    up2 = shift_y(join(up1[:HALF], left0[:D]), 1)
    down2 = shift_y(join(down1[HALF:], right0[ROWS - D :]), -1)
    total = project(
        [c0, up1, down1, right0, left0],
        [
            ((0, 0), [(0, 0, ROWS)]), ((-1, 0), [(1, 0, ROWS)]), ((1, 0), [(2, 0, ROWS)]),
            ((0, -1), [(3, 0, ROWS)]), ((0, 1), [(4, 0, ROWS)]),
        ],
        own_w, other_w, None,
    )
    right1, left1, up2, down2, total = lax.optimization_barrier((right1, left1, up2, down2, total))

    last = join(up2[:HALF], down2[:HALF])
    tail, lower = HALF + ROWS, HALF + ROWS - D
    right2 = shift_x(join(right1[HALF : HALF + MOST], right1[tail : tail + MOST]), 1)
    left2 = shift_x(join(left1[HALF + MOST - D : lower], left1[lower + MOST :], last[E : ROWS - E]), -1)
    up3 = shift_y(join(right1[HALF:ROWS], up2[HALF : HALF + E]), 1)
    down3 = shift_y(join(right1[tail + HALF :], down2[HALF:], left1[lower + ROWS - E :]), -1)
    across2 = shift_x(last, 2)
    total = project(
        [right1, left1, up2, down2],
        [
            ((-1, -1), [(0, HALF, ROWS)]), ((1, -1), [(0, HALF + ROWS, ROWS - D), (3, HALF, D)]),
            ((-1, 1), [(2, HALF, D), (1, HALF, ROWS - D)]), ((1, 1), [(1, lower, ROWS)]),
            ((0, 2), [(0, 0, HALF), (1, 0, HALF)]), ((2, 0), [(2, 0, HALF), (3, 0, HALF)]),
        ],
        own_w, other_w, total,
    )
    right2, left2, across2, up3, down3, total = lax.optimization_barrier(
        (right2, left2, across2, up3, down3, total)
    )
    total = project(
        [right2, left2, across2, up3, down3],
        [
            ((-1, 2), [(0, 0, MOST), (1, 0, REST)]), ((1, 2), [(0, MOST, MOST), (1, REST, REST)]),
            ((2, -1), [(3, 0, HALF), (4, 0, HALF)]), ((2, 2), [(2, 0, ROWS)]),
            ((2, 1), [(3, HALF, E), (1, 2 * REST, ROWS - 2 * E), (4, HALF, E)]),
        ],
        own_w, other_w, total,
    )

    right_a, left_a, across_a, grads = attend(enc_lengths, dec_lengths, total, own_w, other_w)
    right_a, left_a, across_a = shift_x(right_a, 1), shift_x(left_a, -1), shift_x(across_a, 2)
    far, right_b, left_b, up_c, down_c, right_c, left_c, here = spread(grads, own_w, other_w)
    far, right_b, left_b = add_rows(
        [far, right_b, left_b, right_a, left_a, across_a], [N, 2 * N + HS, 2 * N + HS],
        [
            (0, 0, [(0, 0), (3, 0), (4, 0), (5, 0)]), (0, HS, [(0, HS), (3, HS), (4, HS), (5, HS)]),
            (1, 0, [(1, 0), (3, N)]), (1, HS, [(1, HS)]),
            (1, N, [(1, N), (3, N + HS)]), (1, N + HS, [(1, N + HS)]), (1, 2 * N, [(1, 2 * N)]),
            (2, 0, [(2, 0)]), (2, HS, [(2, HS), (4, N)]),
            (2, N, [(2, N)]), (2, N + HS, [(2, N + HS), (4, N + HS)]), (2, 2 * N, [(2, 2 * N)]),
        ],
    )
    far = shift_y(far, 2)
    right_b, left_b = shift_x(right_b, 1), shift_x(left_b, -1)
    up_c, down_c, right_c, left_c = add_rows(
        [up_c, down_c, right_c, left_c, right_b, left_b], [N] * 4,
        [
            (0, 0, [(0, 0), (4, 0), (5, 0)]), (0, HS, [(0, HS), (4, HS), (5, HS)]),
            (1, 0, [(1, 0), (4, N), (5, N)]), (1, HS, [(1, HS), (4, N + HS), (5, N + HS)]),
            (2, 0, [(2, 0), (4, 2 * N)]), (2, HS, [(2, HS)]),
            (3, 0, [(3, 0)]), (3, HS, [(3, HS), (5, 2 * N)]),
        ],
    )
    up_c, down_c, right_c, left_c = shift_y(up_c, 1), shift_y(down_c, -1), shift_x(right_c, 1), shift_x(left_c, -1)
    arrived = [far, up_c, down_c, right_c, left_c]
    sent = add_rows([here, *arrived], [HS], [(0, 0, [(i, HS) for i in range(6)])])[0]
    swapped = lax.ppermute(sent, "section", SWAP)
    return finish(here, arrived, swapped)[None]


def solution(mesh):
    placed = (
        P("section", "dp", "mp"),
        P("section", None, None, "mp"),
        P("dp", "mp"),
        P("dp"),
        P("dp"),
    )
    return jax.shard_map(
        local, mesh=mesh, in_specs=placed, out_specs=P("section", "dp", "mp"), check_vma=False
    )
```

```python
import jax
import jax.numpy as jnp
from jax import lax
from jax.experimental import pallas as pl
from jax.experimental.pallas import tpu as pltpu
from jax.sharding import PartitionSpec as P

HS = 256
SIDE = 4
ROWS = 3 * HS
HALF = ROWS // 2
D = 288
E = 96
MOST = 480
REST = ROWS - MOST
N = 2 * HS
F32 = jnp.float32
BF16 = jnp.bfloat16
SWAP = [(0, 1), (1, 0)]
NT = (((1,), (1,)), ((), ()))
TN = (((0,), (0,)), ((), ()))
VMEM = pl.BlockSpec(memory_space=pltpu.VMEM)
SMEM = pl.BlockSpec(memory_space=pltpu.SMEM)
VMEM_LIMIT = 20 * 2**20


def shift_x(block, step):
    route = [(y * SIDE + x, y * SIDE + (x + step) % SIDE) for y in range(SIDE) for x in range(SIDE)]
    return lax.ppermute(block, "mp", route)


def shift_y(block, step):
    route = [(y * SIDE + x, (y + step) % SIDE * SIDE + x) for y in range(SIDE) for x in range(SIDE)]
    return lax.ppermute(block, "mp", route)


def join(*parts):
    return jnp.concatenate(parts, axis=0)


def call(body, inputs, shapes, flops=0, out_dtype=BF16, scalars=0):
    out = [jax.ShapeDtypeStruct(s, out_dtype) for s in shapes]
    moved = sum(a.size * a.dtype.itemsize for a in inputs)
    return pl.pallas_call(
        body,
        out_shape=out,
        in_specs=[SMEM] * scalars + [VMEM] * (len(inputs) - scalars),
        out_specs=[VMEM] * len(out),
        compiler_params=pltpu.CompilerParams(vmem_limit_bytes=VMEM_LIMIT),
        cost_estimate=pl.CostEstimate(flops=flops, bytes_accessed=moved, transcendentals=0),
    )(*inputs)


def feature_rows(offset):
    me = lax.axis_index("mp")
    y = lax.rem(lax.div(me, SIDE) + offset[0] + SIDE, SIDE)
    x = lax.rem(lax.rem(me, SIDE) + offset[1] + SIDE, SIDE)
    return pl.ds(pl.multiple_of((y * SIDE + x) * HS, HS), HS)


def slot_rows(index):
    return pl.ds(pl.multiple_of(index * HS, HS), HS)


def local_rows(own, cotangent):
    def body(own_ref, cot_ref, out_ref):
        here = slot_rows(lax.axis_index("section"))
        out_ref[:HS, :] = own_ref[here, :]
        out_ref[HS:, :] = cot_ref[here, :]

    return call(body, [own, cotangent], [(N, HS)])[0]


def assemble(local, partner):
    def body(local_ref, partner_ref, out_ref):
        sec = lax.axis_index("section")
        out_ref[:HS, :] = local_ref[:HS, :]
        out_ref[slot_rows(2 - sec), :] = local_ref[HS:, :]
        out_ref[slot_rows(1 + sec), :] = partner_ref[slot_rows(sec), :]

    return call(body, [local, partner], [(ROWS, HS)])[0]


def rows_of(refs, block, low, high):
    parts, at = [], 0
    for which, first, count in block:
        a, b = max(low, at), min(high, at + count)
        if a < b:
            parts.append(refs[which][first + a - at : first + b - at, :])
        at += count
    return parts[0] if len(parts) == 1 else jnp.concatenate(parts, axis=0)


def project(pieces, blocks, own_w, other_w, total):
    def body(u_ref, r_ref, *rest):
        refs, out_ref = rest[: len(pieces)], rest[-1]
        core0 = lax.axis_index("section") == 0
        feats = [feature_rows(offset) for offset, _ in blocks]
        parts = [
            jnp.concatenate([rows_of(refs, block, k * HS, (k + 1) * HS) for _, block in blocks], axis=1)
            for k in range(3)
        ]
        lhs = (parts[0], jnp.where(core0, parts[0], parts[1]), jnp.where(core0, parts[1], parts[2]), parts[2])
        for j in range(4):
            w_ref = (u_ref, r_ref)[j // 2]
            weight = jnp.concatenate([w_ref[j % 2, f, :] for f in feats], axis=0)
            term = jnp.dot(lhs[j], weight, preferred_element_type=F32)
            out_ref[j] = term if total is None else rest[-2][j] + term

    inputs = [own_w, other_w, *pieces] + ([] if total is None else [total])
    return call(body, inputs, [(4, HS, HS)], len(blocks) * 8 * HS**3, F32)[0]


def write_terms(g_ref, u_ref, r_ref, wanted):
    for offset, *slots in wanted:
        feats = feature_rows(offset)
        for slot, (out_ref, row) in enumerate(slots):
            w_ref = (u_ref, r_ref)[slot]
            term = lax.dot_general(g_ref[2 * slot], w_ref[0, feats, :], NT, preferred_element_type=F32)
            term += lax.dot_general(g_ref[2 * slot + 1], w_ref[1, feats, :], NT, preferred_element_type=F32)
            out_ref[row : row + HS, :] = term.astype(BF16)


def attend(enc_lengths, dec_lengths, total, own_w, other_w):
    scale = 1.0 / HS**0.5

    def body(enc_ref, dec_ref, t_ref, u_ref, r_ref, right_ref, left_ref, across_ref, g_ref):
        me = lax.axis_index("section")
        keys = t_ref[2 * me].astype(BF16)
        values = t_ref[2 * me + 1].astype(BF16)
        queries = t_ref[2 - 2 * me].astype(BF16)
        out_grad = t_ref[3 - 2 * me]
        live_q = lax.broadcasted_iota(jnp.int32, (HS, HS), 0) < dec_ref[me]
        live_k = lax.broadcasted_iota(jnp.int32, (HS, HS), 1) < enc_ref[me]
        masked = jnp.where(live_q, out_grad, 0.0).astype(BF16)
        scores = lax.dot_general(queries, keys, NT, preferred_element_type=F32) * scale
        scores = jnp.where(live_k, scores, -1e30)
        top = jnp.max(scores, axis=-1, keepdims=True)
        expd = jnp.exp(scores - top)
        probs = expd / jnp.sum(expd, axis=-1, keepdims=True)
        value_grad = lax.dot_general(probs.astype(BF16), masked, TN, preferred_element_type=F32).astype(BF16)
        prob_grad = lax.dot_general(masked, values, NT, preferred_element_type=F32)
        delta = jnp.sum(probs * prob_grad, axis=-1, keepdims=True)
        sg = (probs * (prob_grad - delta)).astype(BF16)
        query_grad = (jnp.dot(sg, keys, preferred_element_type=F32) * scale).astype(BF16)
        key_grad = (lax.dot_general(sg, queries, TN, preferred_element_type=F32) * scale).astype(BF16)
        g_ref[2 * me] = key_grad
        g_ref[2 * me + 1] = value_grad
        g_ref[2 - 2 * me] = query_grad
        g_ref[3 - 2 * me] = jnp.zeros_like(query_grad)
        write_terms(g_ref, u_ref, r_ref, [
            ((2, 1), (right_ref, 0), (right_ref, HS)),
            ((1, 2), (right_ref, N), (left_ref, N)),
            ((-1, 2), (right_ref, N + HS), (left_ref, N + HS)),
            ((2, -1), (left_ref, 0), (left_ref, HS)),
            ((2, 2), (across_ref, 0), (across_ref, HS)),
        ])

    shapes = [(2 * N, HS), (2 * N, HS), (N, HS), (4, HS, HS)]
    return call(body, [enc_lengths, dec_lengths, total, own_w, other_w], shapes, 60 * HS**3, BF16, 2)


def spread(grads, own_w, other_w):
    def body(g_ref, u_ref, r_ref, far, right, left, up, down, right_c, left_c, here):
        write_terms(g_ref, u_ref, r_ref, [
            ((2, 0), (far, 0), (far, HS)),
            ((1, 1), (right, 0), (right, HS)),
            ((-1, 1), (right, N), (right, N + HS)),
            ((1, -1), (left, 0), (left, HS)),
            ((-1, -1), (left, N), (left, N + HS)),
            ((0, 2), (right, 2 * N), (left, 2 * N)),
            ((1, 0), (up, 0), (up, HS)),
            ((-1, 0), (down, 0), (down, HS)),
            ((0, 1), (right_c, 0), (right_c, HS)),
            ((0, -1), (left_c, 0), (left_c, HS)),
            ((0, 0), (here, 0), (here, HS)),
        ])

    rows = [N, 2 * N + HS, 2 * N + HS, N, N, N, N, N]
    return call(body, [grads, own_w, other_w], [(r, HS) for r in rows], 88 * HS**3)


def add_rows(sources, rows, recipe):
    def body(*refs):
        ins, outs = refs[: len(sources)], refs[len(sources) :]
        for out, row, parts in recipe:
            value = ins[parts[0][0]][parts[0][1] : parts[0][1] + HS, :]
            if len(parts) > 1:
                value = value.astype(F32)
                for source, first in parts[1:]:
                    value += ins[source][first : first + HS, :].astype(F32)
            outs[out][row : row + HS, :] = value.astype(BF16)

    return call(body, list(sources), [(r, HS) for r in rows])


def finish(here, arrived, swapped):
    def body(here_ref, *rest):
        sec = lax.axis_index("section")
        value = here_ref[:HS, :].astype(F32)
        for ref in rest[: len(arrived)]:
            value += ref[:HS, :].astype(F32)
        rest[-1][slot_rows(sec), :] = value.astype(BF16)
        rest[-1][slot_rows(1 - sec), :] = rest[len(arrived)][...]

    return call(body, [here, *arrived, swapped], [(N, HS)])[0]


def local(states, proj_weights, out_cotangent, enc_lengths, dec_lengths):
    own = states[0]
    partner = lax.ppermute(own, "section", SWAP)
    c0 = assemble(local_rows(own, out_cotangent), partner)

    up1, down1 = shift_y(c0, 1), shift_y(c0, -1)
    right0, left0 = shift_x(c0, 1), shift_x(c0, -1)
    c0, up1, down1, right0, left0, own_w = lax.optimization_barrier(
        (c0, up1, down1, right0, left0, proj_weights[0])
    )
    other_w = lax.ppermute(own_w, "section", SWAP)

    right1 = shift_x(join(right0[:HALF], up1, down1[: ROWS - D]), 1)
    left1 = shift_x(join(left0[HALF:], up1[D:], down1), -1)
    up2 = shift_y(join(up1[:HALF], left0[:D]), 1)
    down2 = shift_y(join(down1[HALF:], right0[ROWS - D :]), -1)
    total = project(
        [c0, up1, down1, right0, left0],
        [
            ((0, 0), [(0, 0, ROWS)]), ((-1, 0), [(1, 0, ROWS)]), ((1, 0), [(2, 0, ROWS)]),
            ((0, -1), [(3, 0, ROWS)]), ((0, 1), [(4, 0, ROWS)]),
        ],
        own_w, other_w, None,
    )
    right1, left1, up2, down2, total = lax.optimization_barrier((right1, left1, up2, down2, total))

    last = join(up2[:HALF], down2[:HALF])
    tail, lower = HALF + ROWS, HALF + ROWS - D
    right2 = shift_x(join(right1[HALF : HALF + MOST], right1[tail : tail + MOST]), 1)
    left2 = shift_x(join(left1[HALF + MOST - D : lower], left1[lower + MOST :], last[E : ROWS - E]), -1)
    up3 = shift_y(join(right1[HALF:ROWS], up2[HALF : HALF + E]), 1)
    down3 = shift_y(join(right1[tail + HALF :], down2[HALF:], left1[lower + ROWS - E :]), -1)
    across2 = shift_x(last, 2)
    total = project(
        [right1, left1, up2, down2],
        [
            ((-1, -1), [(0, HALF, ROWS)]), ((1, -1), [(0, HALF + ROWS, ROWS - D), (3, HALF, D)]),
            ((-1, 1), [(2, HALF, D), (1, HALF, ROWS - D)]), ((1, 1), [(1, lower, ROWS)]),
            ((0, 2), [(0, 0, HALF), (1, 0, HALF)]), ((2, 0), [(2, 0, HALF), (3, 0, HALF)]),
        ],
        own_w, other_w, total,
    )
    right2, left2, across2, up3, down3, total = lax.optimization_barrier(
        (right2, left2, across2, up3, down3, total)
    )
    total = project(
        [right2, left2, across2, up3, down3],
        [
            ((-1, 2), [(0, 0, MOST), (1, 0, REST)]), ((1, 2), [(0, MOST, MOST), (1, REST, REST)]),
            ((2, -1), [(3, 0, HALF), (4, 0, HALF)]), ((2, 2), [(2, 0, ROWS)]),
            ((2, 1), [(3, HALF, E), (1, 2 * REST, ROWS - 2 * E), (4, HALF, E)]),
        ],
        own_w, other_w, total,
    )

    right_a, left_a, across_a, grads = attend(enc_lengths, dec_lengths, total, own_w, other_w)
    right_a, left_a, across_a = shift_x(right_a, 1), shift_x(left_a, -1), shift_x(across_a, 2)
    far, right_b, left_b, up_c, down_c, right_c, left_c, here = spread(grads, own_w, other_w)
    far, right_b, left_b = add_rows(
        [far, right_b, left_b, right_a, left_a, across_a], [N, 2 * N + HS, 2 * N + HS],
        [
            (0, 0, [(0, 0), (3, 0), (4, 0), (5, 0)]), (0, HS, [(0, HS), (3, HS), (4, HS), (5, HS)]),
            (1, 0, [(1, 0), (3, N)]), (1, HS, [(1, HS)]),
            (1, N, [(1, N), (3, N + HS)]), (1, N + HS, [(1, N + HS)]), (1, 2 * N, [(1, 2 * N)]),
            (2, 0, [(2, 0)]), (2, HS, [(2, HS), (4, N)]),
            (2, N, [(2, N)]), (2, N + HS, [(2, N + HS), (4, N + HS)]), (2, 2 * N, [(2, 2 * N)]),
        ],
    )
    far = shift_y(far, 2)
    right_b, left_b = shift_x(right_b, 1), shift_x(left_b, -1)
    up_c, down_c, right_c, left_c = add_rows(
        [up_c, down_c, right_c, left_c, right_b, left_b], [N] * 4,
        [
            (0, 0, [(0, 0), (4, 0), (5, 0)]), (0, HS, [(0, HS), (4, HS), (5, HS)]),
            (1, 0, [(1, 0), (4, N), (5, N)]), (1, HS, [(1, HS), (4, N + HS), (5, N + HS)]),
            (2, 0, [(2, 0), (4, 2 * N)]), (2, HS, [(2, HS)]),
            (3, 0, [(3, 0)]), (3, HS, [(3, HS), (5, 2 * N)]),
        ],
    )
    up_c, down_c, right_c, left_c = shift_y(up_c, 1), shift_y(down_c, -1), shift_x(right_c, 1), shift_x(left_c, -1)
    arrived = [far, up_c, down_c, right_c, left_c]
    sent = add_rows([here, *arrived], [HS], [(0, 0, [(i, HS) for i in range(6)])])[0]
    swapped = lax.ppermute(sent, "section", SWAP)
    return finish(here, arrived, swapped)[None]


def solution(mesh):
    placed = (
        P("section", "dp", "mp"),
        P("section", None, None, "mp"),
        P("dp", "mp"),
        P("dp"),
        P("dp"),
    )
    return jax.shard_map(
        local, mesh=mesh, in_specs=placed, out_specs=P("section", "dp", "mp"), check_vma=False
    )
```

```python
import jax
import jax.numpy as jnp
from jax import lax
from jax.experimental import pallas as pl
from jax.experimental.pallas import tpu as pltpu
from jax.sharding import PartitionSpec as P

HS = 256
SIDE = 4
ROWS = 3 * HS
HALF = ROWS // 2
D = 192
E = 96
MOST = 528
REST = ROWS - MOST
N = 2 * HS
F32 = jnp.float32
BF16 = jnp.bfloat16
SWAP = [(0, 1), (1, 0)]
NT = (((1,), (1,)), ((), ()))
TN = (((0,), (0,)), ((), ()))
VMEM = pl.BlockSpec(memory_space=pltpu.VMEM)
SMEM = pl.BlockSpec(memory_space=pltpu.SMEM)
VMEM_LIMIT = 20 * 2**20


def shift_x(block, step):
    route = [(y * SIDE + x, y * SIDE + (x + step) % SIDE) for y in range(SIDE) for x in range(SIDE)]
    return lax.ppermute(block, "mp", route)


def shift_y(block, step):
    route = [(y * SIDE + x, (y + step) % SIDE * SIDE + x) for y in range(SIDE) for x in range(SIDE)]
    return lax.ppermute(block, "mp", route)


def join(*parts):
    return jnp.concatenate(parts, axis=0)


def call(body, inputs, shapes, flops=0, out_dtype=BF16, scalars=0):
    out = [jax.ShapeDtypeStruct(s, out_dtype) for s in shapes]
    moved = sum(a.size * a.dtype.itemsize for a in inputs)
    return pl.pallas_call(
        body,
        out_shape=out,
        in_specs=[SMEM] * scalars + [VMEM] * (len(inputs) - scalars),
        out_specs=[VMEM] * len(out),
        compiler_params=pltpu.CompilerParams(vmem_limit_bytes=VMEM_LIMIT),
        cost_estimate=pl.CostEstimate(flops=flops, bytes_accessed=moved, transcendentals=0),
    )(*inputs)


def feature_rows(offset):
    me = lax.axis_index("mp")
    y = lax.rem(lax.div(me, SIDE) + offset[0] + SIDE, SIDE)
    x = lax.rem(lax.rem(me, SIDE) + offset[1] + SIDE, SIDE)
    return pl.ds(pl.multiple_of((y * SIDE + x) * HS, HS), HS)


def slot_rows(index):
    return pl.ds(pl.multiple_of(index * HS, HS), HS)


def local_rows(own, cotangent):
    def body(own_ref, cot_ref, out_ref):
        here = slot_rows(lax.axis_index("section"))
        out_ref[:HS, :] = own_ref[here, :]
        out_ref[HS:, :] = cot_ref[here, :]

    return call(body, [own, cotangent], [(N, HS)])[0]


def assemble(local, partner):
    def body(local_ref, partner_ref, out_ref):
        sec = lax.axis_index("section")
        out_ref[:HS, :] = local_ref[:HS, :]
        out_ref[slot_rows(2 - sec), :] = local_ref[HS:, :]
        out_ref[slot_rows(1 + sec), :] = partner_ref[slot_rows(sec), :]

    return call(body, [local, partner], [(ROWS, HS)])[0]


def rows_of(refs, block, low, high):
    parts, at = [], 0
    for which, first, count in block:
        a, b = max(low, at), min(high, at + count)
        if a < b:
            parts.append(refs[which][first + a - at : first + b - at, :])
        at += count
    return parts[0] if len(parts) == 1 else jnp.concatenate(parts, axis=0)


def project(pieces, blocks, own_w, other_w, total):
    def body(u_ref, r_ref, *rest):
        refs, out_ref = rest[: len(pieces)], rest[-1]
        core0 = lax.axis_index("section") == 0
        feats = [feature_rows(offset) for offset, _ in blocks]
        parts = [
            jnp.concatenate([rows_of(refs, block, k * HS, (k + 1) * HS) for _, block in blocks], axis=1)
            for k in range(3)
        ]
        lhs = (parts[0], jnp.where(core0, parts[0], parts[1]), jnp.where(core0, parts[1], parts[2]), parts[2])
        for j in range(4):
            w_ref = (u_ref, r_ref)[j // 2]
            weight = jnp.concatenate([w_ref[j % 2, f, :] for f in feats], axis=0)
            term = jnp.dot(lhs[j], weight, preferred_element_type=F32)
            out_ref[j] = term if total is None else rest[-2][j] + term

    inputs = [own_w, other_w, *pieces] + ([] if total is None else [total])
    return call(body, inputs, [(4, HS, HS)], len(blocks) * 8 * HS**3, F32)[0]


def write_terms(g_ref, u_ref, r_ref, wanted):
    for offset, *slots in wanted:
        feats = feature_rows(offset)
        for slot, (out_ref, row) in enumerate(slots):
            w_ref = (u_ref, r_ref)[slot]
            term = lax.dot_general(g_ref[2 * slot], w_ref[0, feats, :], NT, preferred_element_type=F32)
            term += lax.dot_general(g_ref[2 * slot + 1], w_ref[1, feats, :], NT, preferred_element_type=F32)
            out_ref[row : row + HS, :] = term.astype(BF16)


def attend(enc_lengths, dec_lengths, total, own_w, other_w):
    scale = 1.0 / HS**0.5

    def body(enc_ref, dec_ref, t_ref, u_ref, r_ref, right_ref, left_ref, across_ref, g_ref):
        me = lax.axis_index("section")
        keys = t_ref[2 * me].astype(BF16)
        values = t_ref[2 * me + 1].astype(BF16)
        queries = t_ref[2 - 2 * me].astype(BF16)
        out_grad = t_ref[3 - 2 * me]
        live_q = lax.broadcasted_iota(jnp.int32, (HS, HS), 0) < dec_ref[me]
        live_k = lax.broadcasted_iota(jnp.int32, (HS, HS), 1) < enc_ref[me]
        masked = jnp.where(live_q, out_grad, 0.0).astype(BF16)
        scores = lax.dot_general(queries, keys, NT, preferred_element_type=F32) * scale
        scores = jnp.where(live_k, scores, -1e30)
        top = jnp.max(scores, axis=-1, keepdims=True)
        expd = jnp.exp(scores - top)
        probs = expd / jnp.sum(expd, axis=-1, keepdims=True)
        value_grad = lax.dot_general(probs.astype(BF16), masked, TN, preferred_element_type=F32).astype(BF16)
        prob_grad = lax.dot_general(masked, values, NT, preferred_element_type=F32)
        delta = jnp.sum(probs * prob_grad, axis=-1, keepdims=True)
        sg = (probs * (prob_grad - delta)).astype(BF16)
        query_grad = (jnp.dot(sg, keys, preferred_element_type=F32) * scale).astype(BF16)
        key_grad = (lax.dot_general(sg, queries, TN, preferred_element_type=F32) * scale).astype(BF16)
        g_ref[2 * me] = key_grad
        g_ref[2 * me + 1] = value_grad
        g_ref[2 - 2 * me] = query_grad
        g_ref[3 - 2 * me] = jnp.zeros_like(query_grad)
        write_terms(g_ref, u_ref, r_ref, [
            ((2, 1), (right_ref, 0), (right_ref, HS)),
            ((1, 2), (right_ref, N), (left_ref, N)),
            ((-1, 2), (right_ref, N + HS), (left_ref, N + HS)),
            ((2, -1), (left_ref, 0), (left_ref, HS)),
            ((2, 2), (across_ref, 0), (across_ref, HS)),
        ])

    shapes = [(2 * N, HS), (2 * N, HS), (N, HS), (4, HS, HS)]
    return call(body, [enc_lengths, dec_lengths, total, own_w, other_w], shapes, 60 * HS**3, BF16, 2)


def spread(grads, own_w, other_w):
    def body(g_ref, u_ref, r_ref, far, right, left, up, down, right_c, left_c, here):
        write_terms(g_ref, u_ref, r_ref, [
            ((2, 0), (far, 0), (far, HS)),
            ((1, 1), (right, 0), (right, HS)),
            ((-1, 1), (right, N), (right, N + HS)),
            ((1, -1), (left, 0), (left, HS)),
            ((-1, -1), (left, N), (left, N + HS)),
            ((0, 2), (right, 2 * N), (left, 2 * N)),
            ((1, 0), (up, 0), (up, HS)),
            ((-1, 0), (down, 0), (down, HS)),
            ((0, 1), (right_c, 0), (right_c, HS)),
            ((0, -1), (left_c, 0), (left_c, HS)),
            ((0, 0), (here, 0), (here, HS)),
        ])

    rows = [N, 2 * N + HS, 2 * N + HS, N, N, N, N, N]
    return call(body, [grads, own_w, other_w], [(r, HS) for r in rows], 88 * HS**3)


def add_rows(sources, rows, recipe):
    def body(*refs):
        ins, outs = refs[: len(sources)], refs[len(sources) :]
        for out, row, parts in recipe:
            value = ins[parts[0][0]][parts[0][1] : parts[0][1] + HS, :]
            if len(parts) > 1:
                value = value.astype(F32)
                for source, first in parts[1:]:
                    value += ins[source][first : first + HS, :].astype(F32)
            outs[out][row : row + HS, :] = value.astype(BF16)

    return call(body, list(sources), [(r, HS) for r in rows])


def finish(here, arrived, swapped):
    def body(here_ref, *rest):
        sec = lax.axis_index("section")
        value = here_ref[:HS, :].astype(F32)
        for ref in rest[: len(arrived)]:
            value += ref[:HS, :].astype(F32)
        rest[-1][slot_rows(sec), :] = value.astype(BF16)
        rest[-1][slot_rows(1 - sec), :] = rest[len(arrived)][...]

    return call(body, [here, *arrived, swapped], [(N, HS)])[0]


def local(states, proj_weights, out_cotangent, enc_lengths, dec_lengths):
    own = states[0]
    partner = lax.ppermute(own, "section", SWAP)
    c0 = assemble(local_rows(own, out_cotangent), partner)

    up1, down1 = shift_y(c0, 1), shift_y(c0, -1)
    right0, left0 = shift_x(c0, 1), shift_x(c0, -1)
    c0, up1, down1, right0, left0, own_w = lax.optimization_barrier(
        (c0, up1, down1, right0, left0, proj_weights[0])
    )
    other_w = lax.ppermute(own_w, "section", SWAP)

    right1 = shift_x(join(right0[:HALF], up1, down1[: ROWS - D]), 1)
    left1 = shift_x(join(left0[HALF:], up1[D:], down1), -1)
    up2 = shift_y(join(up1[:HALF], left0[:D]), 1)
    down2 = shift_y(join(down1[HALF:], right0[ROWS - D :]), -1)
    total = project(
        [c0, up1, down1, right0, left0],
        [
            ((0, 0), [(0, 0, ROWS)]), ((-1, 0), [(1, 0, ROWS)]), ((1, 0), [(2, 0, ROWS)]),
            ((0, -1), [(3, 0, ROWS)]), ((0, 1), [(4, 0, ROWS)]),
        ],
        own_w, other_w, None,
    )
    right1, left1, up2, down2, total = lax.optimization_barrier((right1, left1, up2, down2, total))

    last = join(up2[:HALF], down2[:HALF])
    tail, lower = HALF + ROWS, HALF + ROWS - D
    right2 = shift_x(join(right1[HALF : HALF + MOST], right1[tail : tail + MOST]), 1)
    left2 = shift_x(join(left1[HALF + MOST - D : lower], left1[lower + MOST :], last[E : ROWS - E]), -1)
    up3 = shift_y(join(right1[HALF:ROWS], up2[HALF : HALF + E]), 1)
    down3 = shift_y(join(right1[tail + HALF :], down2[HALF:], left1[lower + ROWS - E :]), -1)
    across2 = shift_x(last, 2)
    total = project(
        [right1, left1, up2, down2],
        [
            ((-1, -1), [(0, HALF, ROWS)]), ((1, -1), [(0, HALF + ROWS, ROWS - D), (3, HALF, D)]),
            ((-1, 1), [(2, HALF, D), (1, HALF, ROWS - D)]), ((1, 1), [(1, lower, ROWS)]),
            ((0, 2), [(0, 0, HALF), (1, 0, HALF)]), ((2, 0), [(2, 0, HALF), (3, 0, HALF)]),
        ],
        own_w, other_w, total,
    )
    right2, left2, across2, up3, down3, total = lax.optimization_barrier(
        (right2, left2, across2, up3, down3, total)
    )
    total = project(
        [right2, left2, across2, up3, down3],
        [
            ((-1, 2), [(0, 0, MOST), (1, 0, REST)]), ((1, 2), [(0, MOST, MOST), (1, REST, REST)]),
            ((2, -1), [(3, 0, HALF), (4, 0, HALF)]), ((2, 2), [(2, 0, ROWS)]),
            ((2, 1), [(3, HALF, E), (1, 2 * REST, ROWS - 2 * E), (4, HALF, E)]),
        ],
        own_w, other_w, total,
    )

    right_a, left_a, across_a, grads = attend(enc_lengths, dec_lengths, total, own_w, other_w)
    right_a, left_a, across_a = shift_x(right_a, 1), shift_x(left_a, -1), shift_y(across_a, 2)
    far, right_b, left_b, up_c, down_c, right_c, left_c, here = spread(grads, own_w, other_w)
    far, right_b, left_b = add_rows(
        [far, right_b, left_b, right_a, left_a, across_a], [N, 2 * N + HS, 2 * N + HS],
        [
            (0, 0, [(0, 0), (3, 0), (4, 0)]), (0, HS, [(0, HS), (3, HS), (4, HS)]),
            (1, 0, [(1, 0), (3, N)]), (1, HS, [(1, HS)]),
            (1, N, [(1, N), (3, N + HS)]), (1, N + HS, [(1, N + HS)]), (1, 2 * N, [(1, 2 * N), (5, 0)]),
            (2, 0, [(2, 0)]), (2, HS, [(2, HS), (4, N)]),
            (2, N, [(2, N)]), (2, N + HS, [(2, N + HS), (4, N + HS)]), (2, 2 * N, [(2, 2 * N), (5, HS)]),
        ],
    )
    far = shift_y(far, 2)
    right_b, left_b = shift_x(right_b, 1), shift_x(left_b, -1)
    up_c, down_c, right_c, left_c = add_rows(
        [up_c, down_c, right_c, left_c, right_b, left_b], [N] * 4,
        [
            (0, 0, [(0, 0), (4, 0), (5, 0)]), (0, HS, [(0, HS), (4, HS), (5, HS)]),
            (1, 0, [(1, 0), (4, N), (5, N)]), (1, HS, [(1, HS), (4, N + HS), (5, N + HS)]),
            (2, 0, [(2, 0), (4, 2 * N)]), (2, HS, [(2, HS)]),
            (3, 0, [(3, 0)]), (3, HS, [(3, HS), (5, 2 * N)]),
        ],
    )
    up_c, down_c, right_c, left_c = shift_y(up_c, 1), shift_y(down_c, -1), shift_x(right_c, 1), shift_x(left_c, -1)
    arrived = [far, up_c, down_c, right_c, left_c]
    sent = add_rows([here, *arrived], [HS], [(0, 0, [(i, HS) for i in range(6)])])[0]
    swapped = lax.ppermute(sent, "section", SWAP)
    return finish(here, arrived, swapped)[None]


def solution(mesh):
    placed = (
        P("section", "dp", "mp"),
        P("section", None, None, "mp"),
        P("dp", "mp"),
        P("dp"),
        P("dp"),
    )
    return jax.shard_map(
        local, mesh=mesh, in_specs=placed, out_specs=P("section", "dp", "mp"), check_vma=False
    )
```

```python
import jax
import jax.numpy as jnp
from jax import lax
from jax.experimental import pallas as pl
from jax.experimental.pallas import tpu as pltpu
from jax.sharding import PartitionSpec as P

HS = 256
SIDE = 4
ROWS = 3 * HS
HALF = ROWS // 2
D = 192
E = 96
MOST = 528
REST = ROWS - MOST
N = 2 * HS
F32 = jnp.float32
BF16 = jnp.bfloat16
SWAP = [(0, 1), (1, 0)]
NT = (((1,), (1,)), ((), ()))
TN = (((0,), (0,)), ((), ()))
VMEM = pl.BlockSpec(memory_space=pltpu.VMEM)
SMEM = pl.BlockSpec(memory_space=pltpu.SMEM)
VMEM_LIMIT = 20 * 2**20


def shift_x(block, step):
    route = [(y * SIDE + x, y * SIDE + (x + step) % SIDE) for y in range(SIDE) for x in range(SIDE)]
    return lax.ppermute(block, "mp", route)


def shift_y(block, step):
    route = [(y * SIDE + x, (y + step) % SIDE * SIDE + x) for y in range(SIDE) for x in range(SIDE)]
    return lax.ppermute(block, "mp", route)


def join(*parts):
    return jnp.concatenate(parts, axis=0)


def call(body, inputs, shapes, flops=0, out_dtype=BF16, scalars=0):
    out = [jax.ShapeDtypeStruct(s, out_dtype) for s in shapes]
    moved = sum(a.size * a.dtype.itemsize for a in inputs)
    return pl.pallas_call(
        body,
        out_shape=out,
        in_specs=[SMEM] * scalars + [VMEM] * (len(inputs) - scalars),
        out_specs=[VMEM] * len(out),
        compiler_params=pltpu.CompilerParams(vmem_limit_bytes=VMEM_LIMIT),
        cost_estimate=pl.CostEstimate(flops=flops, bytes_accessed=moved, transcendentals=0),
    )(*inputs)


def feature_rows(offset):
    me = lax.axis_index("mp")
    y = lax.rem(lax.div(me, SIDE) + offset[0] + SIDE, SIDE)
    x = lax.rem(lax.rem(me, SIDE) + offset[1] + SIDE, SIDE)
    return pl.ds(pl.multiple_of((y * SIDE + x) * HS, HS), HS)


def slot_rows(index):
    return pl.ds(pl.multiple_of(index * HS, HS), HS)


def local_rows(own, cotangent):
    def body(own_ref, cot_ref, out_ref):
        here = slot_rows(lax.axis_index("section"))
        out_ref[:HS, :] = own_ref[here, :]
        out_ref[HS:, :] = cot_ref[here, :]

    return call(body, [own, cotangent], [(N, HS)])[0]


def assemble(local, partner):
    def body(local_ref, partner_ref, out_ref):
        sec = lax.axis_index("section")
        out_ref[:HS, :] = local_ref[:HS, :]
        out_ref[slot_rows(2 - sec), :] = local_ref[HS:, :]
        out_ref[slot_rows(1 + sec), :] = partner_ref[slot_rows(sec), :]

    return call(body, [local, partner], [(ROWS, HS)])[0]


def rows_of(refs, block, low, high):
    parts, at = [], 0
    for which, first, count in block:
        a, b = max(low, at), min(high, at + count)
        if a < b:
            parts.append(refs[which][first + a - at : first + b - at, :])
        at += count
    return parts[0] if len(parts) == 1 else jnp.concatenate(parts, axis=0)


def project(pieces, blocks, own_w, other_w, total):
    def body(u_ref, r_ref, *rest):
        refs, out_ref = rest[: len(pieces)], rest[-1]
        core0 = lax.axis_index("section") == 0
        feats = [feature_rows(offset) for offset, _ in blocks]
        parts = [
            jnp.concatenate([rows_of(refs, block, k * HS, (k + 1) * HS) for _, block in blocks], axis=1)
            for k in range(3)
        ]
        lhs = (parts[0], jnp.where(core0, parts[0], parts[1]), jnp.where(core0, parts[1], parts[2]), parts[2])
        for j in range(4):
            w_ref = (u_ref, r_ref)[j // 2]
            weight = jnp.concatenate([w_ref[j % 2, f, :] for f in feats], axis=0)
            term = jnp.dot(lhs[j], weight, preferred_element_type=F32)
            out_ref[j] = term if total is None else rest[-2][j] + term

    inputs = [own_w, other_w, *pieces] + ([] if total is None else [total])
    return call(body, inputs, [(4, HS, HS)], len(blocks) * 8 * HS**3, F32)[0]


def write_terms(g_ref, u_ref, r_ref, wanted):
    for offset, *slots in wanted:
        feats = feature_rows(offset)
        for slot, (out_ref, row) in enumerate(slots):
            w_ref = (u_ref, r_ref)[slot]
            term = lax.dot_general(g_ref[2 * slot], w_ref[0, feats, :], NT, preferred_element_type=F32)
            term += lax.dot_general(g_ref[2 * slot + 1], w_ref[1, feats, :], NT, preferred_element_type=F32)
            out_ref[row : row + HS, :] = term.astype(BF16)


def attend(enc_lengths, dec_lengths, total, own_w, other_w):
    scale = 1.0 / HS**0.5

    def body(enc_ref, dec_ref, t_ref, u_ref, r_ref, right_ref, left_ref, across_ref, g_ref):
        me = lax.axis_index("section")
        keys = t_ref[2 * me].astype(BF16)
        values = t_ref[2 * me + 1].astype(BF16)
        queries = t_ref[2 - 2 * me].astype(BF16)
        out_grad = t_ref[3 - 2 * me]
        live_q = lax.broadcasted_iota(jnp.int32, (HS, HS), 0) < dec_ref[me]
        live_k = lax.broadcasted_iota(jnp.int32, (HS, HS), 1) < enc_ref[me]
        masked = jnp.where(live_q, out_grad, 0.0).astype(BF16)
        scores = lax.dot_general(queries, keys, NT, preferred_element_type=F32) * scale
        scores = jnp.where(live_k, scores, -1e30)
        top = jnp.max(scores, axis=-1, keepdims=True)
        expd = jnp.exp(scores - top)
        probs = expd / jnp.sum(expd, axis=-1, keepdims=True)
        value_grad = lax.dot_general(probs.astype(BF16), masked, TN, preferred_element_type=F32).astype(BF16)
        prob_grad = lax.dot_general(masked, values, NT, preferred_element_type=F32)
        delta = jnp.sum(probs * prob_grad, axis=-1, keepdims=True)
        sg = (probs * (prob_grad - delta)).astype(BF16)
        query_grad = (jnp.dot(sg, keys, preferred_element_type=F32) * scale).astype(BF16)
        key_grad = (lax.dot_general(sg, queries, TN, preferred_element_type=F32) * scale).astype(BF16)
        g_ref[2 * me] = key_grad
        g_ref[2 * me + 1] = value_grad
        g_ref[2 - 2 * me] = query_grad
        g_ref[3 - 2 * me] = jnp.zeros_like(query_grad)
        write_terms(g_ref, u_ref, r_ref, [
            ((2, 1), (right_ref, 0), (right_ref, HS)),
            ((1, 2), (right_ref, N), (left_ref, N)),
            ((-1, 2), (right_ref, N + HS), (left_ref, N + HS)),
            ((2, -1), (left_ref, 0), (left_ref, HS)),
            ((2, 2), (across_ref, 0), (across_ref, HS)),
        ])

    shapes = [(2 * N, HS), (2 * N, HS), (N, HS), (4, HS, HS)]
    return call(body, [enc_lengths, dec_lengths, total, own_w, other_w], shapes, 60 * HS**3, BF16, 2)


def spread(grads, own_w, other_w):
    def body(g_ref, u_ref, r_ref, far, right, left, up, down, right_c, left_c, here):
        write_terms(g_ref, u_ref, r_ref, [
            ((2, 0), (far, 0), (far, HS)),
            ((1, 1), (right, 0), (right, HS)),
            ((-1, 1), (right, N), (right, N + HS)),
            ((1, -1), (left, 0), (left, HS)),
            ((-1, -1), (left, N), (left, N + HS)),
            ((0, 2), (right, 2 * N), (left, 2 * N)),
            ((1, 0), (up, 0), (up, HS)),
            ((-1, 0), (down, 0), (down, HS)),
            ((0, 1), (right_c, 0), (right_c, HS)),
            ((0, -1), (left_c, 0), (left_c, HS)),
            ((0, 0), (here, 0), (here, HS)),
        ])

    rows = [N, 2 * N + HS, 2 * N + HS, N, N, N, N, N]
    return call(body, [grads, own_w, other_w], [(r, HS) for r in rows], 88 * HS**3)


def add_rows(sources, rows, recipe):
    def body(*refs):
        ins, outs = refs[: len(sources)], refs[len(sources) :]
        for out, row, parts in recipe:
            value = ins[parts[0][0]][parts[0][1] : parts[0][1] + HS, :]
            if len(parts) > 1:
                value = value.astype(F32)
                for source, first in parts[1:]:
                    value += ins[source][first : first + HS, :].astype(F32)
            outs[out][row : row + HS, :] = value.astype(BF16)

    return call(body, list(sources), [(r, HS) for r in rows])


def finish(here, arrived, swapped):
    def body(here_ref, *rest):
        sec = lax.axis_index("section")
        value = here_ref[:HS, :].astype(F32)
        for ref in rest[: len(arrived)]:
            value += ref[:HS, :].astype(F32)
        rest[-1][slot_rows(sec), :] = value.astype(BF16)
        rest[-1][slot_rows(1 - sec), :] = rest[len(arrived)][...]

    return call(body, [here, *arrived, swapped], [(N, HS)])[0]


def local(states, proj_weights, out_cotangent, enc_lengths, dec_lengths):
    own = states[0]
    partner = lax.ppermute(own, "section", SWAP)
    c0 = assemble(local_rows(own, out_cotangent), partner)

    up1, down1 = shift_y(c0, 1), shift_y(c0, -1)
    right0, left0 = shift_x(c0, 1), shift_x(c0, -1)
    c0, up1, down1, right0, left0, own_w = lax.optimization_barrier(
        (c0, up1, down1, right0, left0, proj_weights[0])
    )
    other_w = lax.ppermute(own_w, "section", SWAP)

    right1 = shift_x(join(right0[:HALF], up1, down1[: ROWS - D]), 1)
    left1 = shift_x(join(left0[HALF:], up1[D:], down1), -1)
    up2 = shift_y(join(up1[:HALF], left0[:D]), 1)
    down2 = shift_y(join(down1[HALF:], right0[ROWS - D :]), -1)
    total = project(
        [c0, up1, down1, right0, left0],
        [
            ((0, 0), [(0, 0, ROWS)]), ((-1, 0), [(1, 0, ROWS)]), ((1, 0), [(2, 0, ROWS)]),
            ((0, -1), [(3, 0, ROWS)]), ((0, 1), [(4, 0, ROWS)]),
        ],
        own_w, other_w, None,
    )
    left1, up2, down2, total = lax.optimization_barrier((left1, up2, down2, total))

    last = join(up2[:HALF], down2[:HALF])
    tail, lower = HALF + ROWS, HALF + ROWS - D
    right2 = shift_x(join(right1[HALF : HALF + MOST], right1[tail : tail + MOST]), 1)
    left2 = shift_x(join(left1[HALF + MOST - D : lower], left1[lower + MOST :], last[E : ROWS - E]), -1)
    up3 = shift_y(join(right1[HALF:ROWS], up2[HALF : HALF + E]), 1)
    down3 = shift_y(join(right1[tail + HALF :], down2[HALF:], left1[lower + ROWS - E :]), -1)
    across2 = shift_x(last, 2)
    total = project(
        [right1, left1, up2, down2],
        [
            ((-1, -1), [(0, HALF, ROWS)]), ((1, -1), [(0, HALF + ROWS, ROWS - D), (3, HALF, D)]),
            ((-1, 1), [(2, HALF, D), (1, HALF, ROWS - D)]), ((1, 1), [(1, lower, ROWS)]),
            ((0, 2), [(0, 0, HALF), (1, 0, HALF)]), ((2, 0), [(2, 0, HALF), (3, 0, HALF)]),
        ],
        own_w, other_w, total,
    )
    right2, left2, across2, up3, down3, total = lax.optimization_barrier(
        (right2, left2, across2, up3, down3, total)
    )
    total = project(
        [right2, left2, across2, up3, down3],
        [
            ((-1, 2), [(0, 0, MOST), (1, 0, REST)]), ((1, 2), [(0, MOST, MOST), (1, REST, REST)]),
            ((2, -1), [(3, 0, HALF), (4, 0, HALF)]), ((2, 2), [(2, 0, ROWS)]),
            ((2, 1), [(3, HALF, E), (1, 2 * REST, ROWS - 2 * E), (4, HALF, E)]),
        ],
        own_w, other_w, total,
    )

    right_a, left_a, across_a, grads = attend(enc_lengths, dec_lengths, total, own_w, other_w)
    right_a, left_a, across_a = shift_x(right_a, 1), shift_x(left_a, -1), shift_x(across_a, 2)
    far, right_b, left_b, up_c, down_c, right_c, left_c, here = spread(grads, own_w, other_w)
    far, right_b, left_b = add_rows(
        [far, right_b, left_b, right_a, left_a, across_a], [N, 2 * N + HS, 2 * N + HS],
        [
            (0, 0, [(0, 0), (3, 0), (4, 0), (5, 0)]), (0, HS, [(0, HS), (3, HS), (4, HS), (5, HS)]),
            (1, 0, [(1, 0), (3, N)]), (1, HS, [(1, HS)]),
            (1, N, [(1, N), (3, N + HS)]), (1, N + HS, [(1, N + HS)]), (1, 2 * N, [(1, 2 * N)]),
            (2, 0, [(2, 0)]), (2, HS, [(2, HS), (4, N)]),
            (2, N, [(2, N)]), (2, N + HS, [(2, N + HS), (4, N + HS)]), (2, 2 * N, [(2, 2 * N)]),
        ],
    )
    far = shift_y(far, 2)
    right_b, left_b = shift_x(right_b, 1), shift_x(left_b, -1)
    up_c, down_c, right_c, left_c = add_rows(
        [up_c, down_c, right_c, left_c, right_b, left_b], [N] * 4,
        [
            (0, 0, [(0, 0), (4, 0), (5, 0)]), (0, HS, [(0, HS), (4, HS), (5, HS)]),
            (1, 0, [(1, 0), (4, N), (5, N)]), (1, HS, [(1, HS), (4, N + HS), (5, N + HS)]),
            (2, 0, [(2, 0), (4, 2 * N)]), (2, HS, [(2, HS)]),
            (3, 0, [(3, 0)]), (3, HS, [(3, HS), (5, 2 * N)]),
        ],
    )
    up_c, down_c, right_c, left_c = shift_y(up_c, 1), shift_y(down_c, -1), shift_x(right_c, 1), shift_x(left_c, -1)
    arrived = [far, up_c, down_c, right_c, left_c]
    sent = add_rows([here, *arrived], [HS], [(0, 0, [(i, HS) for i in range(6)])])[0]
    swapped = lax.ppermute(sent, "section", SWAP)
    return finish(here, arrived, swapped)[None]


def solution(mesh):
    placed = (
        P("section", "dp", "mp"),
        P("section", None, None, "mp"),
        P("dp", "mp"),
        P("dp"),
        P("dp"),
    )
    return jax.shard_map(
        local, mesh=mesh, in_specs=placed, out_specs=P("section", "dp", "mp"), check_vma=False
    )
```

```python
import jax
import jax.numpy as jnp
from jax import lax
from jax.experimental import pallas as pl
from jax.experimental.pallas import tpu as pltpu
from jax.sharding import PartitionSpec as P

HS = 256
SIDE = 4
ROWS = 3 * HS
HALF = ROWS // 2
D = 192
E = 48
MOST = 576
REST = ROWS - MOST
N = 2 * HS
F32 = jnp.float32
BF16 = jnp.bfloat16
SWAP = [(0, 1), (1, 0)]
NT = (((1,), (1,)), ((), ()))
TN = (((0,), (0,)), ((), ()))
VMEM = pl.BlockSpec(memory_space=pltpu.VMEM)
SMEM = pl.BlockSpec(memory_space=pltpu.SMEM)
VMEM_LIMIT = 20 * 2**20


def shift_x(block, step):
    route = [(y * SIDE + x, y * SIDE + (x + step) % SIDE) for y in range(SIDE) for x in range(SIDE)]
    return lax.ppermute(block, "mp", route)


def shift_y(block, step):
    route = [(y * SIDE + x, (y + step) % SIDE * SIDE + x) for y in range(SIDE) for x in range(SIDE)]
    return lax.ppermute(block, "mp", route)


def join(*parts):
    return jnp.concatenate(parts, axis=0)


def call(body, inputs, shapes, flops=0, out_dtype=BF16, scalars=0):
    out = [jax.ShapeDtypeStruct(s, out_dtype) for s in shapes]
    moved = sum(a.size * a.dtype.itemsize for a in inputs)
    return pl.pallas_call(
        body,
        out_shape=out,
        in_specs=[SMEM] * scalars + [VMEM] * (len(inputs) - scalars),
        out_specs=[VMEM] * len(out),
        compiler_params=pltpu.CompilerParams(vmem_limit_bytes=VMEM_LIMIT),
        cost_estimate=pl.CostEstimate(flops=flops, bytes_accessed=moved, transcendentals=0),
    )(*inputs)


def feature_rows(offset):
    me = lax.axis_index("mp")
    y = lax.rem(lax.div(me, SIDE) + offset[0] + SIDE, SIDE)
    x = lax.rem(lax.rem(me, SIDE) + offset[1] + SIDE, SIDE)
    return pl.ds(pl.multiple_of((y * SIDE + x) * HS, HS), HS)


def slot_rows(index):
    return pl.ds(pl.multiple_of(index * HS, HS), HS)


def local_rows(own, cotangent):
    def body(own_ref, cot_ref, out_ref):
        here = slot_rows(lax.axis_index("section"))
        out_ref[:HS, :] = own_ref[here, :]
        out_ref[HS:, :] = cot_ref[here, :]

    return call(body, [own, cotangent], [(N, HS)])[0]


def assemble(local, partner):
    def body(local_ref, partner_ref, out_ref):
        sec = lax.axis_index("section")
        out_ref[:HS, :] = local_ref[:HS, :]
        out_ref[slot_rows(2 - sec), :] = local_ref[HS:, :]
        out_ref[slot_rows(1 + sec), :] = partner_ref[slot_rows(sec), :]

    return call(body, [local, partner], [(ROWS, HS)])[0]


def rows_of(refs, block, low, high):
    parts, at = [], 0
    for which, first, count in block:
        a, b = max(low, at), min(high, at + count)
        if a < b:
            parts.append(refs[which][first + a - at : first + b - at, :])
        at += count
    return parts[0] if len(parts) == 1 else jnp.concatenate(parts, axis=0)


def project(pieces, blocks, own_w, other_w, total):
    def body(u_ref, r_ref, *rest):
        refs, out_ref = rest[: len(pieces)], rest[-1]
        core0 = lax.axis_index("section") == 0
        feats = [feature_rows(offset) for offset, _ in blocks]
        parts = [
            jnp.concatenate([rows_of(refs, block, k * HS, (k + 1) * HS) for _, block in blocks], axis=1)
            for k in range(3)
        ]
        lhs = (parts[0], jnp.where(core0, parts[0], parts[1]), jnp.where(core0, parts[1], parts[2]), parts[2])
        for j in range(4):
            w_ref = (u_ref, r_ref)[j // 2]
            weight = jnp.concatenate([w_ref[j % 2, f, :] for f in feats], axis=0)
            term = jnp.dot(lhs[j], weight, preferred_element_type=F32)
            out_ref[j] = term if total is None else rest[-2][j] + term

    inputs = [own_w, other_w, *pieces] + ([] if total is None else [total])
    return call(body, inputs, [(4, HS, HS)], len(blocks) * 8 * HS**3, F32)[0]


def write_terms(g_ref, u_ref, r_ref, wanted):
    for offset, *slots in wanted:
        feats = feature_rows(offset)
        for slot, (out_ref, row) in enumerate(slots):
            w_ref = (u_ref, r_ref)[slot]
            term = lax.dot_general(g_ref[2 * slot], w_ref[0, feats, :], NT, preferred_element_type=F32)
            term += lax.dot_general(g_ref[2 * slot + 1], w_ref[1, feats, :], NT, preferred_element_type=F32)
            out_ref[row : row + HS, :] = term.astype(BF16)


def attend(enc_lengths, dec_lengths, total, own_w, other_w):
    scale = 1.0 / HS**0.5

    def body(enc_ref, dec_ref, t_ref, u_ref, r_ref, right_ref, left_ref, across_ref, g_ref):
        me = lax.axis_index("section")
        keys = t_ref[2 * me].astype(BF16)
        values = t_ref[2 * me + 1].astype(BF16)
        queries = t_ref[2 - 2 * me].astype(BF16)
        out_grad = t_ref[3 - 2 * me]
        live_q = lax.broadcasted_iota(jnp.int32, (HS, HS), 0) < dec_ref[me]
        live_k = lax.broadcasted_iota(jnp.int32, (HS, HS), 1) < enc_ref[me]
        masked = jnp.where(live_q, out_grad, 0.0).astype(BF16)
        scores = lax.dot_general(queries, keys, NT, preferred_element_type=F32) * scale
        scores = jnp.where(live_k, scores, -1e30)
        top = jnp.max(scores, axis=-1, keepdims=True)
        expd = jnp.exp(scores - top)
        probs = expd / jnp.sum(expd, axis=-1, keepdims=True)
        value_grad = lax.dot_general(probs.astype(BF16), masked, TN, preferred_element_type=F32).astype(BF16)
        prob_grad = lax.dot_general(masked, values, NT, preferred_element_type=F32)
        delta = jnp.sum(probs * prob_grad, axis=-1, keepdims=True)
        sg = (probs * (prob_grad - delta)).astype(BF16)
        query_grad = (jnp.dot(sg, keys, preferred_element_type=F32) * scale).astype(BF16)
        key_grad = (lax.dot_general(sg, queries, TN, preferred_element_type=F32) * scale).astype(BF16)
        g_ref[2 * me] = key_grad
        g_ref[2 * me + 1] = value_grad
        g_ref[2 - 2 * me] = query_grad
        g_ref[3 - 2 * me] = jnp.zeros_like(query_grad)
        write_terms(g_ref, u_ref, r_ref, [
            ((2, 1), (right_ref, 0), (right_ref, HS)),
            ((1, 2), (right_ref, N), (left_ref, N)),
            ((-1, 2), (right_ref, N + HS), (left_ref, N + HS)),
            ((2, -1), (left_ref, 0), (left_ref, HS)),
            ((2, 2), (across_ref, 0), (across_ref, HS)),
        ])

    shapes = [(2 * N, HS), (2 * N, HS), (N, HS), (4, HS, HS)]
    return call(body, [enc_lengths, dec_lengths, total, own_w, other_w], shapes, 60 * HS**3, BF16, 2)


def spread(grads, own_w, other_w):
    def body(g_ref, u_ref, r_ref, far, right, left, up, down, right_c, left_c, here):
        write_terms(g_ref, u_ref, r_ref, [
            ((2, 0), (far, 0), (far, HS)),
            ((1, 1), (right, 0), (right, HS)),
            ((-1, 1), (right, N), (right, N + HS)),
            ((1, -1), (left, 0), (left, HS)),
            ((-1, -1), (left, N), (left, N + HS)),
            ((0, 2), (right, 2 * N), (left, 2 * N)),
            ((1, 0), (up, 0), (up, HS)),
            ((-1, 0), (down, 0), (down, HS)),
            ((0, 1), (right_c, 0), (right_c, HS)),
            ((0, -1), (left_c, 0), (left_c, HS)),
            ((0, 0), (here, 0), (here, HS)),
        ])

    rows = [N, 2 * N + HS, 2 * N + HS, N, N, N, N, N]
    return call(body, [grads, own_w, other_w], [(r, HS) for r in rows], 88 * HS**3)


def add_rows(sources, rows, recipe):
    def body(*refs):
        ins, outs = refs[: len(sources)], refs[len(sources) :]
        for out, row, parts in recipe:
            value = ins[parts[0][0]][parts[0][1] : parts[0][1] + HS, :]
            if len(parts) > 1:
                value = value.astype(F32)
                for source, first in parts[1:]:
                    value += ins[source][first : first + HS, :].astype(F32)
            outs[out][row : row + HS, :] = value.astype(BF16)

    return call(body, list(sources), [(r, HS) for r in rows])


def finish(here, arrived, swapped):
    def body(here_ref, *rest):
        sec = lax.axis_index("section")
        value = here_ref[:HS, :].astype(F32)
        for ref in rest[: len(arrived)]:
            value += ref[:HS, :].astype(F32)
        rest[-1][slot_rows(sec), :] = value.astype(BF16)
        rest[-1][slot_rows(1 - sec), :] = rest[len(arrived)][...]

    return call(body, [here, *arrived, swapped], [(N, HS)])[0]


def local(states, proj_weights, out_cotangent, enc_lengths, dec_lengths):
    own = states[0]
    partner = lax.ppermute(own, "section", SWAP)
    c0 = assemble(local_rows(own, out_cotangent), partner)

    up1, down1 = shift_y(c0, 1), shift_y(c0, -1)
    right0, left0 = shift_x(c0, 1), shift_x(c0, -1)
    c0, up1, down1, right0, left0, own_w = lax.optimization_barrier(
        (c0, up1, down1, right0, left0, proj_weights[0])
    )
    other_w = lax.ppermute(own_w, "section", SWAP)

    right1 = shift_x(join(right0[:HALF], up1, down1[: ROWS - D]), 1)
    left1 = shift_x(join(left0[HALF:], up1[D:], down1), -1)
    up2 = shift_y(join(up1[:HALF], left0[:D]), 1)
    down2 = shift_y(join(down1[HALF:], right0[ROWS - D :]), -1)
    total = project(
        [c0, up1, down1, right0, left0],
        [
            ((0, 0), [(0, 0, ROWS)]), ((-1, 0), [(1, 0, ROWS)]), ((1, 0), [(2, 0, ROWS)]),
            ((0, -1), [(3, 0, ROWS)]), ((0, 1), [(4, 0, ROWS)]),
        ],
        own_w, other_w, None,
    )
    left1, up2, down2, total = lax.optimization_barrier((left1, up2, down2, total))

    last = join(up2[:HALF], down2[:HALF])
    tail, lower = HALF + ROWS, HALF + ROWS - D
    right2 = shift_x(join(right1[HALF : HALF + MOST], right1[tail : tail + MOST]), 1)
    left2 = shift_x(join(left1[HALF + MOST - D : lower], left1[lower + MOST :], last[E : ROWS - E]), -1)
    up3 = shift_y(join(right1[HALF:ROWS], up2[HALF : HALF + E]), 1)
    down3 = shift_y(join(right1[tail + HALF :], down2[HALF:], left1[lower + ROWS - E :]), -1)
    across2 = shift_x(last, 2)
    total = project(
        [right1, left1, up2, down2],
        [
            ((-1, -1), [(0, HALF, ROWS)]), ((1, -1), [(0, HALF + ROWS, ROWS - D), (3, HALF, D)]),
            ((-1, 1), [(2, HALF, D), (1, HALF, ROWS - D)]), ((1, 1), [(1, lower, ROWS)]),
            ((0, 2), [(0, 0, HALF), (1, 0, HALF)]), ((2, 0), [(2, 0, HALF), (3, 0, HALF)]),
        ],
        own_w, other_w, total,
    )
    right2, left2, across2, up3, down3, total = lax.optimization_barrier(
        (right2, left2, across2, up3, down3, total)
    )
    total = project(
        [right2, left2, across2, up3, down3],
        [
            ((-1, 2), [(0, 0, MOST), (1, 0, REST)]), ((1, 2), [(0, MOST, MOST), (1, REST, REST)]),
            ((2, -1), [(3, 0, HALF), (4, 0, HALF)]), ((2, 2), [(2, 0, ROWS)]),
            ((2, 1), [(3, HALF, E), (1, 2 * REST, ROWS - 2 * E), (4, HALF, E)]),
        ],
        own_w, other_w, total,
    )

    right_a, left_a, across_a, grads = attend(enc_lengths, dec_lengths, total, own_w, other_w)
    right_a, left_a, across_a = shift_x(right_a, 1), shift_x(left_a, -1), shift_x(across_a, 2)
    far, right_b, left_b, up_c, down_c, right_c, left_c, here = spread(grads, own_w, other_w)
    far, right_b, left_b = add_rows(
        [far, right_b, left_b, right_a, left_a, across_a], [N, 2 * N + HS, 2 * N + HS],
        [
            (0, 0, [(0, 0), (3, 0), (4, 0), (5, 0)]), (0, HS, [(0, HS), (3, HS), (4, HS), (5, HS)]),
            (1, 0, [(1, 0), (3, N)]), (1, HS, [(1, HS)]),
            (1, N, [(1, N), (3, N + HS)]), (1, N + HS, [(1, N + HS)]), (1, 2 * N, [(1, 2 * N)]),
            (2, 0, [(2, 0)]), (2, HS, [(2, HS), (4, N)]),
            (2, N, [(2, N)]), (2, N + HS, [(2, N + HS), (4, N + HS)]), (2, 2 * N, [(2, 2 * N)]),
        ],
    )
    far = shift_y(far, 2)
    right_b, left_b = shift_x(right_b, 1), shift_x(left_b, -1)
    up_c, down_c, right_c, left_c = add_rows(
        [up_c, down_c, right_c, left_c, right_b, left_b], [N] * 4,
        [
            (0, 0, [(0, 0), (4, 0), (5, 0)]), (0, HS, [(0, HS), (4, HS), (5, HS)]),
            (1, 0, [(1, 0), (4, N), (5, N)]), (1, HS, [(1, HS), (4, N + HS), (5, N + HS)]),
            (2, 0, [(2, 0), (4, 2 * N)]), (2, HS, [(2, HS)]),
            (3, 0, [(3, 0)]), (3, HS, [(3, HS), (5, 2 * N)]),
        ],
    )
    up_c, down_c, right_c, left_c = shift_y(up_c, 1), shift_y(down_c, -1), shift_x(right_c, 1), shift_x(left_c, -1)
    arrived = [far, up_c, down_c, right_c, left_c]
    sent = add_rows([here, *arrived], [HS], [(0, 0, [(i, HS) for i in range(6)])])[0]
    swapped = lax.ppermute(sent, "section", SWAP)
    return finish(here, arrived, swapped)[None]


def solution(mesh):
    placed = (
        P("section", "dp", "mp"),
        P("section", None, None, "mp"),
        P("dp", "mp"),
        P("dp"),
        P("dp"),
    )
    return jax.shard_map(
        local, mesh=mesh, in_specs=placed, out_specs=P("section", "dp", "mp"), check_vma=False
    )
```
